512 devices in a mesh: gz: 4 (over x), row: 16 (over y, core), col: 8 (over z).
Axes of the slice: x: 4, y: 8, z: 8, core: 2. Of those that a mesh axis runs over, the one named last changes fastest.
Arguments:
- root_factor: bfloat16 [12288, 12288], P('row', 'col'), may hold values from -1.5 to 1.5
- partials: bfloat16 [4, 128, 12288], P('gz', 'row', 'col'), may hold values from -3 to 3
- pattern: int32 [48, 48], P('row', 'col'), may hold values 0 or 1
- coupling: bfloat16 [4, 6144, 8192], P('gz', 'row', 'col'), may hold values from -0.0390625 to 0.0390625
- child_factor: bfloat16 [4, 8192, 8192], P('gz', 'row', 'col'), may hold values from -1.5 to 1.5
- child_bits: int32 [4, 128, 8192], P('gz', None, 'col'), may hold values from 0 to 1
Outputs:
- root_adjoint: bfloat16 [128, 12288], P(None, 'row')
- child_adjoint: bfloat16 [4, 128, 8192], P('gz', None, 'row')
The draws below stay inside these ranges and needn't reach their ends.
All inputs are finite; a program needn't handle non-finite values. No bound on the sum of `pattern` on one device may be relied on, other than what follows from the above.
Results may differ from the reference program's by a relative error of at most 0.023.
Values may be sent and summed in bfloat16 or wider, within the bound.
No kernel may reach another device: no remote copies, remote signals or barrier semaphores. Data moves between devices by JAX's collectives and lax.ppermute only.
A program may use at most 64 MiB of HBM per device.

```python
import math
import jax
import jax.numpy as jnp
from jax import lax

S1 = 12288
S2 = 8192
P_SIZE = 128
BLK = 256
CH = 4
RP = 3072
CP = 2048
RB = 768
CB = 512
HALF = 6144
N_ROW = 16
N_COL = 8


def factor_panel(noise, spread, panel_index, panel_size, order):
    rows = panel_index * panel_size + lax.broadcasted_iota(jnp.int32, (panel_size, order), 0)
    cols = lax.broadcasted_iota(jnp.int32, (panel_size, order), 1)
    col_panel = cols // panel_size
    inside = jnp.where(rows > cols, noise * (0.6 / math.sqrt(panel_size)), 0.0)
    inside = jnp.where(rows == cols, 0.7 * jnp.exp2(spread), inside)
    outside = jnp.where(col_panel < panel_index, noise * (0.5 / math.sqrt(order)), 0.0)
    return jnp.where(col_panel == panel_index, inside, outside).astype(jnp.bfloat16)


def draw_root_factor(key, part):
    key = jax.random.fold_in(key, 1)

    def one_panel(index):
        sub_key = jax.random.fold_in(key, index)
        first_key, second_key = jax.random.split(sub_key)
        noise = jnp.clip(jax.random.normal(first_key, (RP, S1), jnp.float32), -4.0, 4.0)
        spread = jax.random.uniform(second_key, (RP, S1), jnp.float32)
        return factor_panel(noise, spread, index, RP, S1)
    return lax.map(one_panel, jnp.arange(S1 // RP)).reshape(S1, S1)


def draw_child_factor(key, part):
    key = jax.random.fold_in(key, 2)
    panel_count = S2 // CP

    def one_panel(index):
        sub_key = jax.random.fold_in(key, index)
        first_key, second_key = jax.random.split(sub_key)
        noise = jnp.clip(jax.random.normal(first_key, (CP, S2), jnp.float32), -4.0, 4.0)
        spread = jax.random.uniform(second_key, (CP, S2), jnp.float32)
        return factor_panel(noise, spread, index % panel_count, CP, S2)
    return lax.map(one_panel, jnp.arange(CH * panel_count)).reshape(CH, S2, S2)


def touch_ends(result, stream_key, smallest, high):
    index_at = [jax.random.randint(jax.random.fold_in(stream_key, axis), (), 0, length) for axis, length in enumerate(result.shape)]
    main_axis = result.shape.index(max(result.shape))
    beside = index_at[:main_axis] + [(index_at[main_axis] + 1) % result.shape[main_axis]] + index_at[main_axis + 1:]
    return result.at[tuple(index_at)].set(smallest).at[tuple(beside)].set(high)


def level_of(own_key, shape, pieces, low, top_value):
    gain = 1.0
    for dim, blocks in pieces:
        heights = jax.random.uniform(jax.random.fold_in(jax.random.fold_in(own_key, 6), dim), (blocks,), jnp.float32, low / len(pieces), top_value / len(pieces))
        gain = gain * jnp.repeat(jnp.exp(heights), shape[dim] // blocks).reshape((-1,) + (1,) * (len(shape) - 1 - dim))
    return gain


def gaussian(own_key, extent, scale, most, shards=(), kind=jnp.bfloat16):
    values = scale * jax.random.normal(own_key, extent, jnp.float32)
    if shards:
        values = values * level_of(own_key, extent, shards, -0.22, 0.18)
    return jnp.clip(values, -most, most).astype(kind)


def setup_inputs(seed: int = 0) -> dict:
    streams_of = jax.random.split(jax.random.key(seed), 7)
    return {
        "root_factor": draw_root_factor(jax.random.fold_in(streams_of[6], 71), 0),
        "partials": gaussian(streams_of[1], (CH, P_SIZE, S1), 0.5, 3.0, ((0, 4), (1, 16), (2, 8))),
        "pattern": touch_ends((jax.random.randint(streams_of[2], (S1 // BLK, S1 // BLK), 0, 4) < 3).astype(jnp.int32), jax.random.fold_in(streams_of[2], 1), 0, 1),
        "coupling": gaussian(streams_of[3], (CH, HALF, S2), (4 * HALF) ** -0.5, 0.0390625, ((0, 4), (1, 16), (2, 8))),
        "child_factor": draw_child_factor(jax.random.fold_in(streams_of[6], 71), 0),
        "child_bits": touch_ends(jax.random.randint(streams_of[5], (CH, P_SIZE, S2), 0, 2), jax.random.fold_in(streams_of[5], 1), 0, 1).astype(jnp.int32),
    }


def solve_panels(factor, right_side, gate, panel, block_rows, col_width):
    order = factor.shape[0]
    count = order // panel
    width = min(col_width, panel)
    probes = right_side.shape[0]
    solved = [None] * count
    for target in range(count - 1, -1, -1):
        low = target * panel
        high = low + panel
        totals = jnp.zeros((probes, panel), jnp.float32)
        for first in range(high, order, block_rows):
            owner = first // panel
            inner = first - owner * panel
            rows_used = solved[owner][:, inner:inner + block_rows]
            block = factor[first:first + block_rows, low:high]
            gate_block = gate[first // BLK:(first + block_rows) // BLK, low // BLK:high // BLK]
            expanded = jnp.repeat(jnp.repeat(gate_block, BLK, 0), BLK, 1).astype(jnp.bfloat16)
            product_term = jnp.dot(rows_used, block * expanded, preferred_element_type=jnp.float32).astype(jnp.bfloat16)
            totals = totals + lax.optimization_barrier(product_term).astype(jnp.float32)
        residual = (right_side[:, low:high] - totals).astype(jnp.bfloat16)
        diagonal = factor[low:high, low:high]
        accum = jnp.zeros((probes, panel), jnp.float32)
        for start in range(0, panel, width):
            piece_term = jnp.dot(residual[:, start:start + width], diagonal[:, start:start + width].T,
                                 preferred_element_type=jnp.float32).astype(jnp.bfloat16)
            accum = accum + lax.optimization_barrier(piece_term).astype(jnp.float32)
        solved[target] = accum.astype(jnp.bfloat16)
    return jnp.concatenate(solved, axis=1)


def reference(root_factor, partials, pattern, coupling, child_factor, child_bits):
    root_rhs = jnp.sum(partials.astype(jnp.float32), axis=0)
    root_adjoint = solve_panels(root_factor, root_rhs, pattern, RP, RB, S1 // N_COL)
    half_block = RB // 2
    all_ones = jnp.ones((S2 // BLK, S2 // BLK), jnp.int32)
    children = []
    for child in range(CH):
        coupled = jnp.zeros((P_SIZE, S2), jnp.float32)
        for block_index in range(N_ROW):
            rows_used = root_adjoint[:, block_index * RB:block_index * RB + half_block]
            weights = coupling[child, block_index * half_block:(block_index + 1) * half_block, :]
            product_term = jnp.dot(rows_used, weights, preferred_element_type=jnp.float32).astype(jnp.bfloat16)
            coupled = coupled + lax.optimization_barrier(product_term).astype(jnp.float32)
        child_rhs = (2 * child_bits[child] - 1).astype(jnp.float32) - coupled
        children.append(solve_panels(child_factor[child], child_rhs, all_ones, CP, CB, S2 // N_COL))
    return root_adjoint, jnp.stack(children)
```

```python
import jax
import jax.numpy as jnp
from jax import lax
from jax.sharding import PartitionSpec as P

PANELS = 4
GROUP = 4
PAIR = 2
ROWS = PANELS * GROUP
COLS = PANELS * PAIR
GRID = ("row", "col")
F32 = jnp.float32
BF16 = jnp.bfloat16


def dot(a, b):
    return jnp.dot(a, b, preferred_element_type=F32)


def dot_t(a, b):
    return lax.dot_general(a, b, (((1,), (1,)), ((), ())), preferred_element_type=F32)


def send(value, moves):
    pairs = []
    for rows, to_rows, row_flip, cols, to_cols, col_flip in moves:
        for j in range(GROUP):
            for q in range(PAIR):
                source = (rows * GROUP + j) * COLS + cols * PAIR + q
                target = (to_rows * GROUP + (j ^ row_flip)) * COLS + to_cols * PAIR + (q ^ col_flip)
                pairs.append((source, target))
    return lax.ppermute(value, GRID, pairs).astype(F32)


def sweep(rhs, forward, diagonal, width, split_rows):
    row_panel = lax.axis_index("row") // GROUP
    col_panel = lax.axis_index("col") // PAIR
    current = jnp.zeros((rhs.shape[0], width), BF16)
    carried = jnp.zeros(rhs.shape, F32)
    totals = jnp.zeros(rhs.shape, F32)
    for r in range(PANELS - 1, -1, -1):
        ahead = None
        if r < PANELS - 1:
            terms = (forward(current) + carried).astype(BF16)
            down = [(r + 1, r, 0, r, r, 0)]
            if r == 1:
                down.append((3, 2, 0, 0, 0, 0))
            first = send(terms, down)
            totals = first
            if split_rows:
                totals = totals + send(terms, [(r + 1, r, 2, r, r, 0)])
            if r >= 1:
                ahead = send(current, [(r + 1, r + 1, 0, r, r - 1, 0)])
            carried = carried + first
        residual = (rhs - totals).astype(BF16)
        piece = diagonal(residual).astype(BF16)
        current = jnp.where((row_panel == r) & (col_panel == r), piece, current)
        if ahead is not None:
            current = (current.astype(F32) + ahead).astype(BF16)
        if r >= 1:
            straight = [(r, r, 0, r, r - 1, 0)]
            crossed = [(r, r, 0, r, r - 1, 1)]
            if r == 2:
                straight.append((3, 3, 0, 1, 0, 0))
                crossed.append((3, 3, 0, 3, 3, 1))
            if r == 1:
                straight.append((2, 2, 0, 0, 3, 0))
                crossed.append((2, 2, 0, 2, 2, 1))
            received = send(current, straight) + send(current, crossed)
            if r < PANELS - 1:
                terms = (forward(current) + carried).astype(BF16)
                carried = carried + send(terms, [(r + 1, r, 0, r - 1, r - 1, 0)])
            current = (current.astype(F32) + received).astype(BF16)
        else:
            received = send(current, [(0, 0, 0, 0, 3, 0), (1, 1, 0, 0, 3, 0)])
            received = received + send(current, [(0, 0, 0, 0, 3, 1), (1, 1, 0, 1, 1, 1)])
            received = received + send(current, [(0, 0, 0, 0, 0, 1)])
            current = (current.astype(F32) + received).astype(BF16)
            received = send(current, [(0, 0, 0, 0, 1, 0), (0, 0, 0, 3, 2, 0), (1, 1, 0, 3, 2, 0)])
            current = (current.astype(F32) + received).astype(BF16)
    return current


def per_device(root_factor, partials, pattern, coupling, child_factor, child_bits):
    layers = lax.axis_size("gz")
    rows_here, cols_here = root_factor.shape
    row_index = lax.axis_index("row")
    col_index = lax.axis_index("col")
    core = row_index % 2
    quarters = [[s * GROUP + j for j in range(GROUP)] for s in range(PANELS)]
    across = [[s * GROUP + j for s in range(PANELS)] for j in range(GROUP)]
    chips = [
        [g * ROWS + 2 * y + k for g in range(layers) for k in range(2)] for y in range(ROWS // 2)
    ]

    with jax.named_scope("mask"):
        block = rows_here // pattern.shape[0]
        expanded = jnp.repeat(jnp.repeat(pattern, block, 0), block, 1)
        on_diagonal = row_index // GROUP == col_index // PAIR
        masked_root = root_factor * jnp.where(on_diagonal, 1, expanded).astype(BF16)
        partner_root = lax.ppermute(masked_root, "row", [(i, i ^ 1) for i in range(ROWS)])

    with jax.named_scope("child_gather"):
        child_panel = lax.all_gather(
            child_factor[0], "row", axis=0, tiled=True, axis_index_groups=quarters
        )

    with jax.named_scope("rhs"):
        probes_here = partials.shape[1]
        lanes = cols_here // 12
        pieces = partials[0].reshape(layers, 1, 2, 12, lanes)
        pieces = jnp.broadcast_to(pieces, (layers, ROWS // 2, 2, 12, lanes))
        pieces = lax.all_to_all(
            pieces.reshape(layers * ROWS, 12, lanes), ("gz", "row"), 0, 0, tiled=True
        )
        root_rhs = jnp.sum(pieces.astype(F32).reshape(layers, ROWS, 12 * lanes), 0)
        root_rhs = root_rhs.astype(BF16).astype(F32)

    with jax.named_scope("root"):
        root_rows = sweep(
            root_rhs,
            lambda x: dot(x[:, :rows_here], masked_root) + dot(x[:, rows_here:], partner_root),
            lambda x: jnp.concatenate([dot_t(x, masked_root), dot_t(x, partner_root)], 1),
            2 * rows_here,
            True,
        )

    with jax.named_scope("coupling"):
        own, other = root_rows[:, :rows_here], root_rows[:, rows_here:]
        by_core = jnp.stack([jnp.where(core == k, own, other) for k in range(2)])
        shared = jnp.broadcast_to(by_core[None], (layers,) + by_core.shape)
        shared = shared.reshape(layers * 2 * ROWS, rows_here)
        shared = lax.all_to_all(shared, ("gz", "row"), 0, 0, tiled=True, axis_index_groups=chips)
        root_all = shared.reshape(layers * 2, ROWS, rows_here).transpose(1, 0, 2)
        root_all = root_all.reshape(layers * 2 * ROWS, rows_here)
        coupled = dot(root_all[:, : rows_here // 2], coupling[0]).astype(BF16)
        coupled = lax.all_to_all(coupled, "row", 0, 0, tiled=True, axis_index_groups=quarters)
        share = coupled.shape[0] // GROUP
        coupled = jnp.sum(coupled.reshape(GROUP, share, -1).astype(F32), 0).astype(BF16)
        coupled = lax.all_gather(coupled, "row", axis=0, axis_index_groups=across)
        coupled = jnp.sum(coupled.astype(F32), 0)
        bits = lax.dynamic_slice_in_dim(child_bits[0], row_index % GROUP * share, share, 0)
        child_rhs = (2 * bits - 1).astype(F32) - coupled

    with jax.named_scope("child"):
        child_rows = sweep(
            child_rhs,
            lambda x: dot(x, child_panel),
            lambda x: dot_t(x, child_panel),
            child_panel.shape[0],
            False,
        )
        child_rows = child_rows.reshape(share, GROUP, -1).transpose(1, 0, 2)
        child_rows = child_rows.reshape(GROUP * share, -1)
        child_rows = lax.all_to_all(child_rows, "row", 0, 0, tiled=True, axis_index_groups=quarters)
    return (root_all, child_rows[None])


def solution(mesh):
    placed = (
        P("row", "col"),
        P("gz", "row", "col"),
        P("row", "col"),
        P("gz", "row", "col"),
        P("gz", "row", "col"),
        P("gz", None, "col"),
    )
    return jax.shard_map(
        per_device,
        mesh=mesh,
        in_specs=placed,
        out_specs=(P(None, "row"), P("gz", None, "row")),
        check_vma=False,
    )
```

```python
import functools

import jax
import jax.numpy as jnp
from jax import lax
from jax.sharding import PartitionSpec as P

PANELS = 4
GROUP = 4
PAIR = 2
ROWS = PANELS * GROUP
COLS = PANELS * PAIR
GRID = ("row", "col")
F32 = jnp.float32
BF16 = jnp.bfloat16


def dot(a, b):
    return jnp.dot(a, b, preferred_element_type=F32)


def dot_t(a, b):
    return lax.dot_general(a, b, (((1,), (1,)), ((), ())), preferred_element_type=F32)


def send(value, moves):
    pairs = []
    for rows, to_rows, row_flip, cols, to_cols, col_flip in moves:
        for j in range(GROUP):
            for q in range(PAIR):
                source = (rows * GROUP + j) * COLS + cols * PAIR + q
                target = (to_rows * GROUP + (j ^ row_flip)) * COLS + to_cols * PAIR + (q ^ col_flip)
                pairs.append((source, target))
    return lax.ppermute(value, GRID, pairs).astype(F32)


def sweep(rhs, forward, diagonal, width, split_rows):
    row_panel = lax.axis_index("row") // GROUP
    col_panel = lax.axis_index("col") // PAIR
    current = jnp.zeros((rhs.shape[0], width), BF16)
    carried = jnp.zeros(rhs.shape, F32)
    totals = jnp.zeros(rhs.shape, F32)
    for r in range(PANELS - 1, -1, -1):
        ahead = None
        if r < PANELS - 1:
            terms = (forward(current) + carried).astype(BF16)
            down = [(r + 1, r, 0, r, r, 0)]
            if r == 1:
                down.append((3, 2, 0, 0, 0, 0))
            first = send(terms, down)
            totals = first
            if split_rows:
                totals = totals + send(terms, [(r + 1, r, 2, r, r, 0)])
            if r >= 1:
                ahead = send(current, [(r + 1, r + 1, 0, r, r - 1, 0)])
            carried = carried + first
        residual = (rhs - totals).astype(BF16)
        piece = diagonal(residual).astype(BF16)
        current = jnp.where((row_panel == r) & (col_panel == r), piece, current)
        if ahead is not None:
            current = (current.astype(F32) + ahead).astype(BF16)
        if r >= 1:
            straight = [(r, r, 0, r, r - 1, 0)]
            crossed = [(r, r, 0, r, r - 1, 1)]
            if r == 2:
                straight.append((3, 3, 0, 1, 0, 0))
                crossed.append((3, 3, 0, 3, 3, 1))
            if r == 1:
                straight.append((2, 2, 0, 0, 3, 0))
                crossed.append((2, 2, 0, 2, 2, 1))
            received = send(current, straight) + send(current, crossed)
            if r < PANELS - 1:
                terms = (forward(current) + carried).astype(BF16)
                carried = carried + send(terms, [(r + 1, r, 0, r - 1, r - 1, 0)])
            current = (current.astype(F32) + received).astype(BF16)
        else:
            received = send(current, [(0, 0, 0, 0, 3, 0), (1, 1, 0, 0, 3, 0)])
            received = received + send(current, [(0, 0, 0, 0, 3, 1), (1, 1, 0, 1, 1, 1)])
            received = received + send(current, [(0, 0, 0, 0, 0, 1)])
            current = (current.astype(F32) + received).astype(BF16)
            received = send(current, [(0, 0, 0, 0, 1, 0), (0, 0, 0, 3, 2, 0), (1, 1, 0, 3, 2, 0)])
            current = (current.astype(F32) + received).astype(BF16)
    return current


def home_sweep(rhs, forward, diagonal, width, then):
    row_panel = lax.axis_index("row") // GROUP
    col_panel = lax.axis_index("col") // PAIR
    current = jnp.zeros((rhs.shape[0], width), BF16)
    carried = jnp.zeros(rhs.shape, F32)
    for r in range(PANELS - 1, -1, -1):
        home = (r + 1) % PANELS
        ahead = None
        if r == 2:
            ahead = send(current, [(3, 3, 0, 2, 1, 0)])
        if r == 1:
            ahead = send(current, [(2, 2, 0, 1, 0, 0), (3, 3, 0, 1, 0, 0)])
        if r < PANELS - 1:
            residual = (rhs - (forward(current) + carried)).astype(BF16)
        else:
            residual = rhs.astype(BF16)
        piece = diagonal(residual).astype(BF16)
        if r == 1:
            piece, then = lax.optimization_barrier((piece, then))
        shown = jnp.where((row_panel == home) & (col_panel == r), piece, current)
        if r >= 1:
            straight = [(home, r, 0, r, r - 1, 0)]
            if r == 1:
                straight.append((3, 3, 0, 2, 3, 0))
            received = send(shown, straight) + send(shown, [(home, r, 0, r, r - 1, 1)])
            if ahead is not None:
                current = (current.astype(F32) + ahead).astype(BF16)
                terms = forward(current).astype(BF16)
                carried = send(terms, [(r + 1, r, 0, r - 1, r - 1, 0)])
                if r == 1:
                    carried = carried + send(terms, [(3, 1, 0, 0, 0, 0)])
            current = (current.astype(F32) + received).astype(BF16)
        else:
            received = send(shown, [(1, 0, 0, 0, 3, 0), (2, 2, 0, 1, 2, 0)])
            received = received + send(shown, [(1, 0, 0, 0, 3, 1), (2, 2, 0, 0, 3, 0)])
            received = received + send(shown, [(1, 0, 0, 0, 0, 0)])
            received = received + send(shown, [(1, 0, 0, 0, 0, 1)])
            received = received + send(current, [(1, 1, 0, 0, 1, 0)])
            received = received + send(current, [(1, 1, 0, 0, 3, 0)])
            current = (current.astype(F32) + received).astype(BF16)
            received = send(current, [(0, 0, 0, 0, 1, 0), (0, 0, 0, 3, 2, 0), (1, 1, 0, 1, 2, 0)])
            current = (current.astype(F32) + received).astype(BF16)
    return current, then


def per_device(root_factor, partials, pattern, coupling, child_factor, child_bits):
    layers = lax.axis_size("gz")
    rows_here, cols_here = root_factor.shape
    row_index = lax.axis_index("row")
    col_index = lax.axis_index("col")
    core = row_index % 2
    quarters = [[s * GROUP + j for j in range(GROUP)] for s in range(PANELS)]
    panels = [
        [g * ROWS + s * GROUP + j for g in range(layers) for j in range(GROUP)] for s in range(PANELS)
    ]
    chips = [
        [g * ROWS + 2 * y + k for g in range(layers) for k in range(2)] for y in range(ROWS // 2)
    ]

    with jax.named_scope("mask"):
        swap = [(i, i ^ 1) for i in range(ROWS)]
        partner_factor = lax.ppermute(root_factor, "row", swap)
        partner_pattern = lax.ppermute(pattern, "row", swap)
        block = rows_here // pattern.shape[0]
        on_diagonal = row_index // GROUP == col_index // PAIR

        def masked(factor, blocks):
            expanded = jnp.repeat(jnp.repeat(blocks, block, 0), block, 1)
            return factor * jnp.where(on_diagonal, 1, expanded).astype(BF16)

        masked_root = masked(root_factor, pattern)
        partner_root = masked(partner_factor, partner_pattern)

    with jax.named_scope("gathers"):
        pairs = [
            ((r * GROUP + j) * COLS + r * PAIR + q, ((r + 1) % PANELS * GROUP + j) * COLS + r * PAIR + q)
            for r in range(PANELS)
            for j in range(GROUP)
            for q in range(PAIR)
        ]
        gather = functools.partial(
            lax.all_gather, axis_name="row", axis=0, tiled=True, axis_index_groups=quarters
        )
        coupling_panel = gather(coupling[0])
        child_diagonal = gather(lax.ppermute(child_factor[0], GRID, pairs))
        child_panel = gather(child_factor[0])

    with jax.named_scope("rhs"):
        probes_here = partials.shape[1]
        lanes = cols_here // 12
        pieces = partials[0].reshape(layers, 1, 2, 12, lanes)
        pieces = jnp.broadcast_to(pieces, (layers, ROWS // 2, 2, 12, lanes))
        pieces = lax.all_to_all(
            pieces.reshape(layers * ROWS, 12, lanes), ("gz", "row"), 0, 0, tiled=True
        )
        root_rhs = jnp.sum(pieces.astype(F32).reshape(layers, ROWS, 12 * lanes), 0)
        root_rhs = root_rhs.astype(BF16).astype(F32)

    with jax.named_scope("root"):
        root_rows = sweep(
            root_rhs,
            lambda x: dot(x[:, :rows_here], masked_root) + dot(x[:, rows_here:], partner_root),
            lambda x: jnp.concatenate([dot_t(x, masked_root), dot_t(x, partner_root)], 1),
            2 * rows_here,
            True,
        )

    with jax.named_scope("coupling"):
        own, other = root_rows[:, :rows_here], root_rows[:, rows_here:]
        half = rows_here // 2
        own_half, other_half = own[:, :half], other[:, :half]
        halves = jnp.where(
            core == 0,
            jnp.concatenate([own_half, other_half], 1),
            jnp.concatenate([other_half, own_half], 1),
        )
        some = ROWS // GROUP
        shared = jnp.broadcast_to(
            halves.reshape(1, GROUP, some, rows_here), (layers, GROUP, some, rows_here)
        )
        shared = lax.all_to_all(
            shared.reshape(layers * GROUP, some, rows_here),
            ("gz", "row"),
            0,
            0,
            tiled=True,
            axis_index_groups=panels,
        )
        shared = shared.reshape(layers, 2, 2, some, rows_here).transpose(3, 0, 2, 1, 4)
        share = some * layers * 2
        terms = dot(shared.reshape(share, 2 * rows_here), coupling_panel).astype(BF16)
        coupled = terms.astype(F32)
        for d in range(1, PANELS):
            coupled = coupled + send(
                terms, [((p + 1 + d) % PANELS, (p + 1) % PANELS, 0, p, p, 0) for p in range(PANELS)]
            )
        bits = lax.dynamic_slice_in_dim(child_bits[0], row_index % GROUP * share, share, 0)
        child_rhs = (2 * bits - 1).astype(F32) - coupled

    with jax.named_scope("child"):
        by_core = jnp.stack([jnp.where(core == k, own, other) for k in range(2)])
        child_rows, by_core = home_sweep(
            child_rhs,
            lambda x: dot(x, child_panel),
            lambda x: dot_t(x, child_diagonal),
            child_panel.shape[0],
            by_core,
        )
        child_rows = child_rows.reshape(share, GROUP, -1).transpose(1, 0, 2)
        child_rows = child_rows.reshape(GROUP * share, -1)
        child_rows = lax.all_to_all(child_rows, "row", 0, 0, tiled=True, axis_index_groups=quarters)

    with jax.named_scope("root_out"):
        shared = jnp.broadcast_to(by_core[None], (layers,) + by_core.shape)
        shared = shared.reshape(layers * 2 * ROWS, rows_here)
        shared = lax.all_to_all(shared, ("gz", "row"), 0, 0, tiled=True, axis_index_groups=chips)
        root_all = shared.reshape(layers * 2, ROWS, rows_here).transpose(1, 0, 2)
        root_all = root_all.reshape(layers * 2 * ROWS, rows_here)
    return (root_all, child_rows[None])


def solution(mesh):
    placed = (
        P("row", "col"),
        P("gz", "row", "col"),
        P("row", "col"),
        P("gz", "row", "col"),
        P("gz", "row", "col"),
        P("gz", None, "col"),
    )
    return jax.shard_map(
        per_device,
        mesh=mesh,
        in_specs=placed,
        out_specs=(P(None, "row"), P("gz", None, "row")),
        check_vma=False,
    )
```

```python
import jax
import jax.numpy as jnp
from jax import lax
from jax.sharding import PartitionSpec as P

PANELS = 4
GROUP = 4
PAIR = 2
ROWS = PANELS * GROUP
COLS = PANELS * PAIR
GRID = ("row", "col")
F32 = jnp.float32
BF16 = jnp.bfloat16


def dot(a, b):
    return jnp.dot(a, b, preferred_element_type=F32)


def dot_t(a, b):
    return lax.dot_general(a, b, (((1,), (1,)), ((), ())), preferred_element_type=F32)


def send(value, moves):
    pairs = []
    for rows, to_rows, row_flip, cols, to_cols, col_flip in moves:
        for j in range(GROUP):
            for q in range(PAIR):
                source = (rows * GROUP + j) * COLS + cols * PAIR + q
                target = (to_rows * GROUP + (j ^ row_flip)) * COLS + to_cols * PAIR + (q ^ col_flip)
                pairs.append((source, target))
    return lax.ppermute(value, GRID, pairs).astype(F32)


def sweep(rhs, own, other, then=None):
    rows = own.shape[0]

    def forward(x):
        return dot(x[:, :rows], own) + dot(x[:, rows:], other)

    def diagonal(x):
        return jnp.concatenate([dot_t(x, own), dot_t(x, other)], 1)

    row_panel = lax.axis_index("row") // GROUP
    col_panel = lax.axis_index("col") // PAIR
    current = jnp.zeros((rhs.shape[0], 2 * rows), BF16)
    carried = jnp.zeros(rhs.shape, F32)
    totals = jnp.zeros(rhs.shape, F32)
    for r in range(PANELS - 1, -1, -1):
        ahead = None
        if r < PANELS - 1:
            terms = (forward(current) + carried).astype(BF16)
            down = [(r + 1, r, 0, r, r, 0)]
            if r == 1:
                down.append((3, 2, 0, 0, 0, 0))
            first = send(terms, down)
            totals = first + send(terms, [(r + 1, r, 2, r, r, 0)])
            if r >= 1:
                ahead = send(current, [(r + 1, r + 1, 0, r, r - 1, 0)])
            carried = carried + first
        residual = (rhs - totals).astype(BF16)
        piece = diagonal(residual).astype(BF16)
        if r == 1 and then is not None:
            piece, then = lax.optimization_barrier((piece, then))
        current = jnp.where((row_panel == r) & (col_panel == r), piece, current)
        if ahead is not None:
            current = (current.astype(F32) + ahead).astype(BF16)
        if r >= 1:
            straight = [(r, r, 0, r, r - 1, 0)]
            crossed = [(r, r, 0, r, r - 1, 1)]
            if r == 2:
                straight.append((3, 3, 0, 1, 0, 0))
                crossed.append((3, 3, 0, 3, 3, 1))
            if r == 1:
                straight.append((2, 2, 0, 0, 3, 0))
                crossed.append((2, 2, 0, 2, 2, 1))
            received = send(current, straight) + send(current, crossed)
            if r < PANELS - 1:
                terms = (forward(current) + carried).astype(BF16)
                carried = carried + send(terms, [(r + 1, r, 0, r - 1, r - 1, 0)])
            current = (current.astype(F32) + received).astype(BF16)
        else:
            received = send(current, [(0, 0, 0, 0, 3, 0), (1, 1, 0, 0, 3, 0)])
            received = received + send(current, [(0, 0, 0, 0, 3, 1), (1, 1, 0, 1, 1, 1)])
            received = received + send(current, [(0, 0, 0, 0, 0, 1)])
            current = (current.astype(F32) + received).astype(BF16)
            received = send(current, [(0, 0, 0, 0, 1, 0), (0, 0, 0, 3, 2, 0), (1, 1, 0, 3, 2, 0)])
            current = (current.astype(F32) + received).astype(BF16)
    return current[:, :rows], current[:, rows:], then


def per_device(root_factor, partials, pattern, coupling, child_factor, child_bits):
    layers = lax.axis_size("gz")
    rows_here, cols_here = root_factor.shape
    row_index = lax.axis_index("row")
    col_index = lax.axis_index("col")
    core = row_index % 2
    quarters = [[s * GROUP + j for j in range(GROUP)] for s in range(PANELS)]
    panels = [
        [g * ROWS + s * GROUP + j for g in range(layers) for j in range(GROUP)] for s in range(PANELS)
    ]
    chips = [
        [g * ROWS + 2 * y + k for g in range(layers) for k in range(2)] for y in range(ROWS // 2)
    ]

    with jax.named_scope("mask"):
        swap = [(i, i ^ 1) for i in range(ROWS)]
        partner_factor = lax.ppermute(root_factor, "row", swap)
        partner_pattern = lax.ppermute(pattern, "row", swap)
        block = rows_here // pattern.shape[0]
        on_diagonal = row_index // GROUP == col_index // PAIR

        def masked(factor, blocks):
            expanded = jnp.repeat(jnp.repeat(blocks, block, 0), block, 1)
            return factor * jnp.where(on_diagonal, 1, expanded).astype(BF16)

        masked_root = masked(root_factor, pattern)
        partner_root = masked(partner_factor, partner_pattern)

        partner_child = lax.ppermute(child_factor[0], "row", swap)

    with jax.named_scope("rhs"):
        probes_here = partials.shape[1]
        lanes = cols_here // 12
        pieces = partials[0].reshape(layers, 1, 2, 12, lanes)
        pieces = jnp.broadcast_to(pieces, (layers, ROWS // 2, 2, 12, lanes))
        pieces = lax.all_to_all(
            pieces.reshape(layers * ROWS, 12, lanes), ("gz", "row"), 0, 0, tiled=True
        )
        root_rhs = jnp.sum(pieces.astype(F32).reshape(layers, ROWS, 12 * lanes), 0)
        root_rhs = root_rhs.astype(BF16).astype(F32)

    with jax.named_scope("gather"):
        coupling_here, root_rhs, partner_child = lax.optimization_barrier(
            (coupling[0], root_rhs, partner_child)
        )
        coupling_panel = lax.all_gather(
            coupling_here, "row", axis=0, tiled=True, axis_index_groups=quarters
        )

    with jax.named_scope("root"):
        own, other, _ = sweep(root_rhs, masked_root, partner_root)

    with jax.named_scope("coupling"):
        half = rows_here // 2
        own_half, other_half = own[:, :half], other[:, :half]
        halves = jnp.where(
            core == 0,
            jnp.concatenate([own_half, other_half], 1),
            jnp.concatenate([other_half, own_half], 1),
        )
        some = ROWS // 2
        shared = jnp.broadcast_to(
            halves.reshape(1, 1, 2, some, rows_here), (layers, 2, 2, some, rows_here)
        )
        shared = lax.all_to_all(
            shared.reshape(layers * GROUP, some, rows_here),
            ("gz", "row"),
            0,
            0,
            tiled=True,
            axis_index_groups=panels,
        )
        shared = shared.reshape(layers, 2, 2, some, rows_here).transpose(3, 0, 2, 1, 4)
        share = some * layers * 2
        terms = dot(shared.reshape(share, 2 * rows_here), coupling_panel).astype(BF16)
        coupled = terms.astype(F32)
        for d in range(1, PANELS):
            coupled = coupled + send(terms, [((p + d) % PANELS, p, 0, p, p, 0) for p in range(PANELS)])
        bits = lax.dynamic_slice_in_dim(child_bits[0], core * share, share, 0)
        child_rhs = (2 * bits - 1).astype(F32) - coupled

    with jax.named_scope("child"):
        by_core = jnp.stack([jnp.where(core == k, own, other) for k in range(2)])
        own, other, by_core = sweep(child_rhs, child_factor[0], partner_child, by_core)
        other = lax.ppermute(other, "row", swap)
        child_rows = jnp.where(
            core == 0, jnp.concatenate([own, other], 0), jnp.concatenate([other, own], 0)
        )

    with jax.named_scope("root_out"):
        shared = jnp.broadcast_to(by_core[None], (layers,) + by_core.shape)
        shared = shared.reshape(layers * 2 * ROWS, rows_here)
        shared = lax.all_to_all(shared, ("gz", "row"), 0, 0, tiled=True, axis_index_groups=chips)
        root_all = shared.reshape(layers * 2, ROWS, rows_here).transpose(1, 0, 2)
        root_all = root_all.reshape(layers * 2 * ROWS, rows_here)
    return (root_all, child_rows[None])


def solution(mesh):
    placed = (
        P("row", "col"),
        P("gz", "row", "col"),
        P("row", "col"),
        P("gz", "row", "col"),
        P("gz", "row", "col"),
        P("gz", None, "col"),
    )
    return jax.shard_map(
        per_device,
        mesh=mesh,
        in_specs=placed,
        out_specs=(P(None, "row"), P("gz", None, "row")),
        check_vma=False,
    )
```

```python
import jax
import jax.numpy as jnp
from jax import lax
from jax.sharding import PartitionSpec as P

PANELS = 4
GROUP = 4
PAIR = 2
ROWS = PANELS * GROUP
COLS = PANELS * PAIR
GRID = ("row", "col")
F32 = jnp.float32
BF16 = jnp.bfloat16


def dot(a, b):
    return jnp.dot(a, b, preferred_element_type=F32)


def dot_t(a, b):
    return lax.dot_general(a, b, (((1,), (1,)), ((), ())), preferred_element_type=F32)


def send(value, moves):
    pairs = []
    for rows, to_rows, row_flip, cols, to_cols, col_flip in moves:
        for j in range(GROUP):
            for q in range(PAIR):
                source = (rows * GROUP + j) * COLS + cols * PAIR + q
                target = (to_rows * GROUP + (j ^ row_flip)) * COLS + to_cols * PAIR + (q ^ col_flip)
                pairs.append((source, target))
    return lax.ppermute(value, GRID, pairs).astype(F32)


def sweep(rhs, own, other, split_rows):
    rows = own.shape[0]

    def forward(x):
        return dot(x[:, :rows], own) + dot(x[:, rows:], other)

    def diagonal(x):
        return jnp.concatenate([dot_t(x, own), dot_t(x, other)], 1)

    row_panel = lax.axis_index("row") // GROUP
    col_panel = lax.axis_index("col") // PAIR
    current = jnp.zeros((rhs.shape[0], 2 * rows), BF16)
    carried = jnp.zeros(rhs.shape, F32)
    totals = jnp.zeros(rhs.shape, F32)
    for r in range(PANELS - 1, -1, -1):
        ahead = None
        if r < PANELS - 1:
            terms = (forward(current) + carried).astype(BF16)
            down = [(r + 1, r, 0, r, r, 0)]
            if r == 1:
                down.append((3, 2, 0, 0, 0, 0))
            first = send(terms, down)
            totals = first
            if split_rows:
                totals = totals + send(terms, [(r + 1, r, 2, r, r, 0)])
            if r >= 1:
                ahead = send(current, [(r + 1, r + 1, 0, r, r - 1, 0)])
            carried = carried + first
        residual = (rhs - totals).astype(BF16)
        piece = diagonal(residual).astype(BF16)
        current = jnp.where((row_panel == r) & (col_panel == r), piece, current)
        if ahead is not None:
            current = (current.astype(F32) + ahead).astype(BF16)
        if r >= 1:
            straight = [(r, r, 0, r, r - 1, 0)]
            crossed = [(r, r, 0, r, r - 1, 1)]
            if r == 2:
                straight.append((3, 3, 0, 1, 0, 0))
                crossed.append((3, 3, 0, 3, 3, 1))
            if r == 1:
                straight.append((2, 2, 0, 0, 3, 0))
                crossed.append((2, 2, 0, 2, 2, 1))
            received = send(current, straight) + send(current, crossed)
            if r < PANELS - 1:
                terms = (forward(current) + carried).astype(BF16)
                carried = carried + send(terms, [(r + 1, r, 0, r - 1, r - 1, 0)])
            current = (current.astype(F32) + received).astype(BF16)
        else:
            received = send(current, [(0, 0, 0, 0, 3, 0), (1, 1, 0, 0, 3, 0)])
            received = received + send(current, [(0, 0, 0, 0, 3, 1), (1, 1, 0, 1, 1, 1)])
            received = received + send(current, [(0, 0, 0, 0, 0, 1)])
            current = (current.astype(F32) + received).astype(BF16)
            received = send(current, [(0, 0, 0, 0, 1, 0), (0, 0, 0, 3, 2, 0), (1, 1, 0, 3, 2, 0)])
            current = (current.astype(F32) + received).astype(BF16)
    return current[:, :rows], current[:, rows:]


def per_device(root_factor, partials, pattern, coupling, child_factor, child_bits):
    layers = lax.axis_size("gz")
    rows_here, cols_here = root_factor.shape
    row_index = lax.axis_index("row")
    col_index = lax.axis_index("col")
    core = row_index % 2
    quarters = [[s * GROUP + j for j in range(GROUP)] for s in range(PANELS)]
    opposite = [[s * GROUP + k, s * GROUP + 2 + k] for s in range(PANELS) for k in range(2)]
    chips = [
        [g * ROWS + 2 * y + k for g in range(layers) for k in range(2)] for y in range(ROWS // 2)
    ]

    with jax.named_scope("mask"):
        swap = [(i, i ^ 1) for i in range(ROWS)]
        partner_factor = lax.ppermute(root_factor, "row", swap)
        partner_pattern = lax.ppermute(pattern, "row", swap)
        block = rows_here // pattern.shape[0]
        on_diagonal = row_index // GROUP == col_index // PAIR

        def masked(factor, blocks):
            expanded = jnp.repeat(jnp.repeat(blocks, block, 0), block, 1)
            return factor * jnp.where(on_diagonal, 1, expanded).astype(BF16)

        masked_root = masked(root_factor, pattern)
        partner_root = masked(partner_factor, partner_pattern)


    with jax.named_scope("rhs"):
        probes_here = partials.shape[1]
        lanes = cols_here // 12
        pieces = partials[0].reshape(layers, 1, 2, 12, lanes)
        pieces = jnp.broadcast_to(pieces, (layers, ROWS // 2, 2, 12, lanes))
        pieces = lax.all_to_all(
            pieces.reshape(layers * ROWS, 12, lanes), ("gz", "row"), 0, 0, tiled=True
        )
        root_rhs = jnp.sum(pieces.astype(F32).reshape(layers, ROWS, 12, lanes), 0)
        root_rhs = root_rhs.astype(BF16).reshape(ROWS, 12 * lanes).astype(F32)

    with jax.named_scope("child_gather"):
        child_own = lax.all_gather(
            child_factor[0], "row", axis=0, tiled=True, axis_index_groups=opposite
        )

    with jax.named_scope("root"):
        own, other = sweep(root_rhs, masked_root, partner_root, True)

    with jax.named_scope("coupling"):
        by_core = jnp.stack([jnp.where(core == k, own, other) for k in range(2)])
        by_core, child_own = lax.optimization_barrier((by_core, child_own))
        child_other = lax.ppermute(child_own, "row", swap)
        shared = jnp.broadcast_to(by_core[None], (layers,) + by_core.shape)
        shared = shared.reshape(layers * 2 * ROWS, rows_here)
        shared = lax.all_to_all(shared, ("gz", "row"), 0, 0, tiled=True, axis_index_groups=chips)
        root_all = shared.reshape(layers * 2, ROWS, rows_here).transpose(1, 0, 2)
        root_all = root_all.reshape(layers * 2 * ROWS, rows_here)
        terms = dot(root_all[:, : rows_here // 2], coupling[0]).astype(BF16)
        terms = lax.all_to_all(terms, "row", 0, 0, tiled=True, axis_index_groups=quarters)
        share = terms.shape[0] // GROUP
        terms = jnp.sum(terms.reshape(GROUP, share, -1).astype(F32), 0).astype(BF16)
        coupled = terms.astype(F32)
        for d in range(1, PANELS):
            coupled = coupled + send(terms, [((p + d) % PANELS, p, 0, p, p, 0) for p in range(PANELS)])
        bits = lax.dynamic_slice_in_dim(child_bits[0], row_index % GROUP * share, share, 0)
        child_rhs = (2 * bits - 1).astype(F32) - coupled

    with jax.named_scope("child"):
        own, other = sweep(child_rhs, child_own, child_other, False)
        blocks = jnp.stack(
            [jnp.where(core == k, own, other).reshape(share, 2, -1) for k in range(2)], 2
        )
        child_rows = blocks.reshape(share, GROUP, -1).transpose(1, 0, 2)
        child_rows = child_rows.reshape(GROUP * share, -1)
        child_rows = lax.all_to_all(child_rows, "row", 0, 0, tiled=True, axis_index_groups=quarters)
    return (root_all, child_rows[None])


def solution(mesh):
    placed = (
        P("row", "col"),
        P("gz", "row", "col"),
        P("row", "col"),
        P("gz", "row", "col"),
        P("gz", "row", "col"),
        P("gz", None, "col"),
    )
    return jax.shard_map(
        per_device,
        mesh=mesh,
        in_specs=placed,
        out_specs=(P(None, "row"), P("gz", None, "row")),
        check_vma=False,
    )
```

```python
import jax
import jax.numpy as jnp
from jax import lax
from jax.sharding import PartitionSpec as P

PANELS = 4
GROUP = 4
PAIR = 2
ROWS = PANELS * GROUP
COLS = PANELS * PAIR
GRID = ("row", "col")
F32 = jnp.float32
BF16 = jnp.bfloat16


def dot(a, b):
    return jnp.dot(a, b, preferred_element_type=F32)


def dot_t(a, b):
    return lax.dot_general(a, b, (((1,), (1,)), ((), ())), preferred_element_type=F32)


def send(value, moves):
    pairs = []
    for rows, to_rows, row_flip, cols, to_cols, col_flip in moves:
        for j in range(GROUP):
            for q in range(PAIR):
                source = (rows * GROUP + j) * COLS + cols * PAIR + q
                target = (to_rows * GROUP + (j ^ row_flip)) * COLS + to_cols * PAIR + (q ^ col_flip)
                pairs.append((source, target))
    return lax.ppermute(value, GRID, pairs).astype(F32)


def sweep(rhs, blocks, split_rows, beside=lambda r, value: value):
    rows = blocks[0].shape[0]

    def forward(x):
        return sum(dot(x[:, i * rows : (i + 1) * rows], block) for i, block in enumerate(blocks))

    def diagonal(x):
        return jnp.concatenate([dot_t(x, block) for block in blocks], 1)

    row_panel = lax.axis_index("row") // GROUP
    col_panel = lax.axis_index("col") // PAIR
    current = jnp.zeros((rhs.shape[0], len(blocks) * rows), BF16)
    carried = jnp.zeros(rhs.shape, F32)
    totals = jnp.zeros(rhs.shape, F32)
    for r in range(PANELS - 1, -1, -1):
        ahead = None
        if r < PANELS - 1:
            terms = beside(r, (forward(current) + carried).astype(BF16))
            down = [(r + 1, r, 0, r, r, 0)]
            if r == 1:
                down.append((3, 2, 0, 0, 0, 0))
            first = send(terms, down)
            totals = first
            if split_rows:
                totals = totals + send(terms, [(r + 1, r, 2, r, r, 0)])
            if r >= 1:
                ahead = send(current, [(r + 1, r + 1, 0, r, r - 1, 0)])
            carried = carried + first
        residual = (rhs - totals).astype(BF16)
        piece = diagonal(residual).astype(BF16)
        if r == PANELS - 1:
            piece = beside(r, piece)
        current = jnp.where((row_panel == r) & (col_panel == r), piece, current)
        if ahead is not None:
            current = (current.astype(F32) + ahead).astype(BF16)
        if r >= 1:
            straight = [(r, r, 0, r, r - 1, 0)]
            crossed = [(r, r, 0, r, r - 1, 1)]
            if r == 2:
                straight.append((3, 3, 0, 1, 0, 0))
                crossed.append((3, 3, 0, 3, 3, 1))
            if r == 1:
                straight.append((2, 2, 0, 0, 3, 0))
                crossed.append((2, 2, 0, 2, 2, 1))
            received = send(current, straight) + send(current, crossed)
            if r < PANELS - 1:
                terms = (forward(current) + carried).astype(BF16)
                carried = carried + send(terms, [(r + 1, r, 0, r - 1, r - 1, 0)])
            current = (current.astype(F32) + received).astype(BF16)
        else:
            received = send(current, [(0, 0, 0, 0, 3, 0), (1, 1, 0, 0, 3, 0)])
            received = received + send(current, [(0, 0, 0, 0, 3, 1), (1, 1, 0, 1, 1, 1)])
            received = received + send(current, [(0, 0, 0, 0, 0, 1)])
            current = (current.astype(F32) + received).astype(BF16)
            received = send(current, [(0, 0, 0, 0, 1, 0), (0, 0, 0, 3, 2, 0), (1, 1, 0, 3, 2, 0)])
            current = (current.astype(F32) + received).astype(BF16)
    return current


def per_device(root_factor, partials, pattern, coupling, child_factor, child_bits):
    layers = lax.axis_size("gz")
    rows_here, cols_here = root_factor.shape
    row_index = lax.axis_index("row")
    col_index = lax.axis_index("col")
    core = row_index % 2
    quarters = [[s * GROUP + j for j in range(GROUP)] for s in range(PANELS)]
    chips = [
        [g * ROWS + 2 * y + k for g in range(layers) for k in range(2)] for y in range(ROWS // 2)
    ]

    with jax.named_scope("mask"):
        swap = [(i, i ^ 1) for i in range(ROWS)]
        partner_factor = lax.ppermute(root_factor, "row", swap)
        partner_pattern = lax.ppermute(pattern, "row", swap)
        block = rows_here // pattern.shape[0]
        on_diagonal = row_index // GROUP == col_index // PAIR

        def masked(factor, blocks):
            expanded = jnp.repeat(jnp.repeat(blocks, block, 0), block, 1)
            return factor * jnp.where(on_diagonal, 1, expanded).astype(BF16)

        masked_root = masked(root_factor, pattern)
        partner_root = masked(partner_factor, partner_pattern)


    with jax.named_scope("rhs"):
        probes_here = partials.shape[1]
        lanes = cols_here // 12
        pieces = partials[0].reshape(layers, 1, 2, 12, lanes)
        pieces = jnp.broadcast_to(pieces, (layers, ROWS // 2, 2, 12, lanes))
        pieces = lax.all_to_all(
            pieces.reshape(layers * ROWS, 12, lanes), ("gz", "row"), 0, 0, tiled=True
        )
        root_rhs = jnp.sum(pieces.astype(F32).reshape(layers, ROWS, 12, lanes), 0)
        root_rhs = root_rhs.astype(BF16).reshape(ROWS, 12 * lanes).astype(F32)

    child_here = child_factor[0]
    moved = {}

    def rows_of(half, flip):
        first = half * ROWS // 2
        return [(i, i ^ flip) for i in range(first, first + ROWS // 2)]

    def move_children(r, value):
        if r == 1:
            value, moved[0, 1], there = lax.optimization_barrier((value, moved[0, 1], moved[0, 2]))
            moved[0, 2] = there
            moved[0, 3] = lax.ppermute(there, "row", rows_of(0, 1))
        if r == 0:
            value, moved[0, 3] = lax.optimization_barrier((value, moved[0, 3]))
        if r == 3 or r == 0:
            half = 0 if r == 3 else 1
            value, here = lax.optimization_barrier((value, child_here))
            moved[half, 2] = lax.ppermute(here, "row", rows_of(half, 2))
            moved[half, 1] = lax.ppermute(here, "row", rows_of(half, 1))
        return value

    with jax.named_scope("root"):
        root_rows = sweep(root_rhs, [masked_root, partner_root], True, move_children)

    with jax.named_scope("coupling"):
        root_rows, there = lax.optimization_barrier((root_rows, moved[1, 2]))
        moved[1, 3] = lax.ppermute(there, "row", rows_of(1, 1))
        own, other = root_rows[:, :rows_here], root_rows[:, rows_here:]
        by_core = jnp.stack([jnp.where(core == k, own, other) for k in range(2)])
        shared = jnp.broadcast_to(by_core[None], (layers,) + by_core.shape)
        shared = shared.reshape(layers * 2 * ROWS, rows_here)
        shared = lax.all_to_all(shared, ("gz", "row"), 0, 0, tiled=True, axis_index_groups=chips)
        root_all = shared.reshape(layers * 2, ROWS, rows_here).transpose(1, 0, 2)
        root_all = root_all.reshape(layers * 2 * ROWS, rows_here)
        terms = dot(root_all[:, : rows_here // 2], coupling[0]).astype(BF16)
        terms = lax.all_to_all(terms, "row", 0, 0, tiled=True, axis_index_groups=quarters)
        share = terms.shape[0] // GROUP
        terms = jnp.sum(terms.reshape(GROUP, share, -1).astype(F32), 0).astype(BF16)
        coupled = terms.astype(F32)
        for d in range(1, PANELS):
            coupled = coupled + send(terms, [((p + d) % PANELS, p, 0, p, p, 0) for p in range(PANELS)])
        bits = lax.dynamic_slice_in_dim(child_bits[0], row_index % GROUP * share, share, 0)
        child_rhs = (2 * bits - 1).astype(F32) - coupled

    with jax.named_scope("child"):
        blocks = [child_here] + [moved[0, flip] + moved[1, flip] for flip in (1, 2, 3)]
        child_rows = sweep(child_rhs, blocks, False).reshape(share, 2, 2, -1)
        child_rows = jnp.where(core == 1, child_rows[:, :, ::-1], child_rows)
        child_rows = jnp.where(row_index % GROUP // 2 == 1, child_rows[:, ::-1], child_rows)
        child_rows = child_rows.reshape(share, GROUP, -1).transpose(1, 0, 2)
        child_rows = child_rows.reshape(GROUP * share, -1)
        child_rows = lax.all_to_all(child_rows, "row", 0, 0, tiled=True, axis_index_groups=quarters)
    return (root_all, child_rows[None])


def solution(mesh):
    placed = (
        P("row", "col"),
        P("gz", "row", "col"),
        P("row", "col"),
        P("gz", "row", "col"),
        P("gz", "row", "col"),
        P("gz", None, "col"),
    )
    return jax.shard_map(
        per_device,
        mesh=mesh,
        in_specs=placed,
        out_specs=(P(None, "row"), P("gz", None, "row")),
        check_vma=False,
    )
```

```python
import jax
import jax.numpy as jnp
from jax import lax
from jax.experimental import pallas as pl
from jax.experimental.pallas import tpu as pltpu
from jax.sharding import PartitionSpec as P

PANELS = 4
GROUP = 4
PAIR = 2
ROWS = PANELS * GROUP
COLS = PANELS * PAIR
GRID = ("row", "col")
F32 = jnp.float32
BF16 = jnp.bfloat16


def dot(a, b):
    return jnp.dot(a, b, preferred_element_type=F32)


def dot_t(a, b):
    return lax.dot_general(a, b, (((1,), (1,)), ((), ())), preferred_element_type=F32)


def send(value, moves):
    pairs = []
    for rows, to_rows, row_flip, cols, to_cols, col_flip in moves:
        for j in range(GROUP):
            for q in range(PAIR):
                source = (rows * GROUP + j) * COLS + cols * PAIR + q
                target = (to_rows * GROUP + (j ^ row_flip)) * COLS + to_cols * PAIR + (q ^ col_flip)
                pairs.append((source, target))
    return lax.ppermute(value, GRID, pairs)


def terms_kernel(keep_own, keep_other, x, own, other, carried, terms, total):
    step = pl.program_id(0)
    block = own.shape[0]

    @pl.when(step == 0)
    def _():
        total[...] = carried[...]

    for c in range(own.shape[1] // block):
        cols = slice(c * block, (c + 1) * block)
        total[:, cols] += keep_own[step, c] * dot(x[0], own[:, cols])
        total[:, cols] += keep_other[step, c] * dot(x[1], other[:, cols])

    @pl.when(step == pl.num_programs(0) - 1)
    def _():
        terms[...] = total[...].astype(BF16)


def root_terms(keep, factors, current, carried):
    steps, probes, (rows, cols) = keep[0].shape[0], current.shape[1], factors[0].shape
    factor_spec = pl.BlockSpec((rows // steps, cols), lambda i: (i, 0))
    whole = pl.BlockSpec((probes, cols), lambda i: (0, 0))
    return pl.pallas_call(
        terms_kernel,
        grid=(steps,),
        in_specs=[pl.BlockSpec(memory_space=pltpu.SMEM)] * 2
        + [pl.BlockSpec((2, probes, rows // steps), lambda i: (0, 0, i))]
        + [factor_spec] * 2
        + [whole],
        out_specs=whole,
        out_shape=jax.ShapeDtypeStruct((probes, cols), BF16),
        scratch_shapes=[pltpu.VMEM((probes, cols), F32)],
        compiler_params=pltpu.CompilerParams(vmem_limit_bytes=8 * 2**20),
        cost_estimate=pl.CostEstimate(
            flops=4 * probes * rows * cols, bytes_accessed=4 * rows * cols, transcendentals=0
        ),
    )(*keep, *([current] + list(factors) + [carried]))


def pieces_kernel(solving, rhs, first, second, own, other, current, out, residual):
    @pl.when(pl.program_id(0) == 0)
    def _():
        totals = first[...].astype(F32) + second[...].astype(F32)
        residual[...] = (rhs[...] - totals).astype(BF16)

    for k, factor in enumerate((own, other)):
        piece = dot_t(residual[...], factor[...])
        out[k] = jnp.where(solving[0] == 1, piece, current[k].astype(F32)).astype(BF16)


def root_pieces(solving, rhs, first, second, factors, current):
    (rows, cols), probes, steps = factors[0].shape, rhs.shape[0], 3
    factor_spec = pl.BlockSpec((rows // steps, cols), lambda i: (i, 0))
    whole = pl.BlockSpec((probes, cols), lambda i: (0, 0))
    part = pl.BlockSpec((2, probes, rows // steps), lambda i: (0, 0, i))
    return pl.pallas_call(
        pieces_kernel,
        grid=(steps,),
        in_specs=[pl.BlockSpec(memory_space=pltpu.SMEM)] + [whole] * 3 + [factor_spec] * 2 + [part],
        out_specs=part,
        out_shape=jax.ShapeDtypeStruct(current.shape, BF16),
        scratch_shapes=[pltpu.VMEM((probes, cols), BF16)],
        compiler_params=pltpu.CompilerParams(vmem_limit_bytes=8 * 2**20),
        cost_estimate=pl.CostEstimate(
            flops=4 * probes * rows * cols, bytes_accessed=4 * rows * cols, transcendentals=0
        ),
    )(solving.astype(jnp.int32).reshape(1), rhs, first, second, *factors, current)


def sweep(rhs, current, forward, solve, split_rows, beside=lambda r, value: value):
    row_panel = lax.axis_index("row") // GROUP
    col_panel = lax.axis_index("col") // PAIR
    carried = jnp.zeros(rhs.shape, F32)
    first = second = jnp.zeros(rhs.shape, BF16)
    for r in range(PANELS - 1, -1, -1):
        ahead = None
        if r < PANELS - 1:
            terms = beside(r, forward(current, carried))
            down = [(r + 1, r, 0, r, r, 0)]
            if r == 1:
                down.append((3, 2, 0, 0, 0, 0))
            first = send(terms, down)
            if split_rows:
                second = send(terms, [(r + 1, r, 2, r, r, 0)])
            if r >= 1:
                ahead = send(current, [(r + 1, r + 1, 0, r, r - 1, 0)])
            carried = carried + first.astype(F32)
        current = solve((row_panel == r) & (col_panel == r), rhs, first, second, current)
        if r == PANELS - 1:
            current = beside(r, current)
        if ahead is not None:
            current = (current.astype(F32) + ahead.astype(F32)).astype(BF16)
        if r >= 1:
            straight = [(r, r, 0, r, r - 1, 0)]
            crossed = [(r, r, 0, r, r - 1, 1)]
            if r == 2:
                straight.append((3, 3, 0, 1, 0, 0))
                crossed.append((3, 3, 0, 3, 3, 1))
            if r == 1:
                straight.append((2, 2, 0, 0, 3, 0))
                crossed.append((2, 2, 0, 2, 2, 1))
            received = send(current, straight).astype(F32) + send(current, crossed).astype(F32)
            if r < PANELS - 1:
                terms = forward(current, carried)
                carried = carried + send(terms, [(r + 1, r, 0, r - 1, r - 1, 0)]).astype(F32)
            current = (current.astype(F32) + received).astype(BF16)
        else:
            received = [
                send(current, [(0, 0, 0, 0, 3, 0), (1, 1, 0, 0, 3, 0)]),
                send(current, [(0, 0, 0, 0, 3, 1), (1, 1, 0, 1, 1, 1)]),
                send(current, [(0, 0, 0, 0, 0, 1)]),
            ]
            current = sum([part.astype(F32) for part in received], current.astype(F32)).astype(BF16)
            received = send(current, [(0, 0, 0, 0, 1, 0), (0, 0, 0, 3, 2, 0), (1, 1, 0, 3, 2, 0)])
            current = (current.astype(F32) + received.astype(F32)).astype(BF16)
    return current


def per_device(root_factor, partials, pattern, coupling, child_factor, child_bits):
    layers = lax.axis_size("gz")
    rows_here, cols_here = root_factor.shape
    row_index = lax.axis_index("row")
    col_index = lax.axis_index("col")
    core = row_index % 2
    quarters = [[s * GROUP + j for j in range(GROUP)] for s in range(PANELS)]
    chips = [
        [g * ROWS + 2 * y + k for g in range(layers) for k in range(2)] for y in range(ROWS // 2)
    ]

    with jax.named_scope("mask"):
        swap = [(i, i ^ 1) for i in range(ROWS)]
        partner_factor = lax.ppermute(root_factor, "row", swap)
        partner_pattern = lax.ppermute(pattern, "row", swap)
        on_diagonal = row_index // GROUP == col_index // PAIR
        keep = [jnp.where(on_diagonal, 1, p).astype(F32) for p in (pattern, partner_pattern)]
        factors = [root_factor, partner_factor]

    with jax.named_scope("rhs"):
        probes_here = partials.shape[1]
        lanes = cols_here // 12
        pieces = partials[0].reshape(layers, 1, 2, 12, lanes)
        pieces = jnp.broadcast_to(pieces, (layers, ROWS // 2, 2, 12, lanes))
        pieces = lax.all_to_all(
            pieces.reshape(layers * ROWS, 12, lanes), ("gz", "row"), 0, 0, tiled=True
        )
        root_rhs = jnp.sum(pieces.astype(F32).reshape(layers, ROWS, 12, lanes), 0)
        root_rhs = root_rhs.astype(BF16).reshape(ROWS, 12 * lanes).astype(F32)

    child_here = child_factor[0]
    moved = {}

    def rows_of(half, flip):
        first = half * ROWS // 2
        return [(i, i ^ flip) for i in range(first, first + ROWS // 2)]

    def move_children(r, value):
        if r == 1:
            value, moved[0, 1], there = lax.optimization_barrier((value, moved[0, 1], moved[0, 2]))
            moved[0, 2] = there
            moved[0, 3] = lax.ppermute(there, "row", rows_of(0, 1))
        if r == 0:
            value, moved[0, 3] = lax.optimization_barrier((value, moved[0, 3]))
        if r == 3 or r == 0:
            half = 0 if r == 3 else 1
            value, here = lax.optimization_barrier((value, child_here))
            moved[half, 2] = lax.ppermute(here, "row", rows_of(half, 2))
            moved[half, 1] = lax.ppermute(here, "row", rows_of(half, 1))
        return value

    with jax.named_scope("root"):
        root_rows = sweep(
            root_rhs,
            jnp.zeros((2, root_rhs.shape[0], rows_here), BF16),
            lambda current, carried: root_terms(keep, factors, current, carried),
            lambda solving, rhs, first, second, current: root_pieces(
                solving, rhs, first, second, factors, current
            ),
            True,
            move_children,
        )

    with jax.named_scope("coupling"):
        root_rows, there = lax.optimization_barrier((root_rows, moved[1, 2]))
        moved[1, 3] = lax.ppermute(there, "row", rows_of(1, 1))
        own, other = root_rows[0], root_rows[1]
        by_core = jnp.stack([jnp.where(core == k, own, other) for k in range(2)])
        shared = jnp.broadcast_to(by_core[None], (layers,) + by_core.shape)
        shared = shared.reshape(layers * 2 * ROWS, rows_here)
        shared = lax.all_to_all(shared, ("gz", "row"), 0, 0, tiled=True, axis_index_groups=chips)
        root_all = shared.reshape(layers * 2, ROWS, rows_here).transpose(1, 0, 2)
        root_all = root_all.reshape(layers * 2 * ROWS, rows_here)
        terms = dot(root_all[:, : rows_here // 2], coupling[0]).astype(BF16)
        terms = lax.all_to_all(terms, "row", 0, 0, tiled=True, axis_index_groups=quarters)
        share = terms.shape[0] // GROUP
        terms = jnp.sum(terms.reshape(GROUP, share, -1).astype(F32), 0).astype(BF16)
        coupled = terms.astype(F32)
        for d in range(1, PANELS):
            parts = [((p + d) % PANELS, p, 0, p, p, 0) for p in range(PANELS)]
            coupled = coupled + send(terms, parts).astype(F32)
        bits = lax.dynamic_slice_in_dim(child_bits[0], row_index % GROUP * share, share, 0)
        child_rhs = (2 * bits - 1).astype(F32) - coupled

    with jax.named_scope("child"):
        blocks = [child_here] + [moved[0, flip] + moved[1, flip] for flip in (1, 2, 3)]
        rows = child_here.shape[0]

        def child_terms(current, carried):
            for i, block in enumerate(blocks):
                carried = carried + dot(current[:, i * rows : (i + 1) * rows], block)
            return carried.astype(BF16)

        def child_pieces(solving, rhs, first, second, current):
            residual = (rhs - first.astype(F32)).astype(BF16)
            piece = jnp.concatenate([dot_t(residual, block) for block in blocks], 1).astype(BF16)
            return jnp.where(solving, piece, current)

        child_rows = jnp.zeros((share, GROUP * rows), BF16)
        child_rows = sweep(child_rhs, child_rows, child_terms, child_pieces, False)
        child_rows = child_rows.reshape(share, 2, 2, -1)
        child_rows = jnp.where(core == 1, child_rows[:, :, ::-1], child_rows)
        child_rows = jnp.where(row_index % GROUP // 2 == 1, child_rows[:, ::-1], child_rows)
        child_rows = child_rows.reshape(share, GROUP, -1).transpose(1, 0, 2)
        child_rows = child_rows.reshape(GROUP * share, -1)
        child_rows = lax.all_to_all(child_rows, "row", 0, 0, tiled=True, axis_index_groups=quarters)
    return (root_all, child_rows[None])


def solution(mesh):
    placed = (
        P("row", "col"),
        P("gz", "row", "col"),
        P("row", "col"),
        P("gz", "row", "col"),
        P("gz", "row", "col"),
        P("gz", None, "col"),
    )
    return jax.shard_map(
        per_device,
        mesh=mesh,
        in_specs=placed,
        out_specs=(P(None, "row"), P("gz", None, "row")),
        check_vma=False,
    )
```

```python
import jax
import jax.numpy as jnp
from jax import lax
from jax.experimental import pallas as pl
from jax.experimental.pallas import tpu as pltpu
from jax.sharding import PartitionSpec as P

PANELS = 4
GROUP = 4
PAIR = 2
ROWS = PANELS * GROUP
COLS = PANELS * PAIR
GRID = ("row", "col")
F32 = jnp.float32
BF16 = jnp.bfloat16


def dot(a, b):
    return jnp.dot(a, b, preferred_element_type=F32)


def dot_t(a, b):
    return lax.dot_general(a, b, (((1,), (1,)), ((), ())), preferred_element_type=F32)


def send(value, moves):
    pairs = []
    for rows, to_rows, row_flip, cols, to_cols, col_flip in moves:
        for j in range(GROUP):
            for q in range(PAIR):
                source = (rows * GROUP + j) * COLS + cols * PAIR + q
                target = (to_rows * GROUP + (j ^ row_flip)) * COLS + to_cols * PAIR + (q ^ col_flip)
                pairs.append((source, target))
    return lax.ppermute(value, GRID, pairs)


def terms_kernel(keep_own, keep_other, x, own, other, carried, terms, total):
    step = pl.program_id(0)
    block = own.shape[0]

    @pl.when(step == 0)
    def _():
        total[...] = carried[...]

    for c in range(own.shape[1] // block):
        cols = slice(c * block, (c + 1) * block)
        total[:, cols] += keep_own[step, c] * dot(x[0], own[:, cols])
        total[:, cols] += keep_other[step, c] * dot(x[1], other[:, cols])

    @pl.when(step == pl.num_programs(0) - 1)
    def _():
        terms[...] = total[...].astype(BF16)


def root_terms(keep, factors, current, carried):
    steps, probes, (rows, cols) = keep[0].shape[0], current.shape[1], factors[0].shape
    factor_spec = pl.BlockSpec((rows // steps, cols), lambda i: (i, 0))
    whole = pl.BlockSpec((probes, cols), lambda i: (0, 0))
    return pl.pallas_call(
        terms_kernel,
        grid=(steps,),
        in_specs=[pl.BlockSpec(memory_space=pltpu.SMEM)] * 2
        + [pl.BlockSpec((2, probes, rows // steps), lambda i: (0, 0, i))]
        + [factor_spec] * 2
        + [whole],
        out_specs=whole,
        out_shape=jax.ShapeDtypeStruct((probes, cols), BF16),
        scratch_shapes=[pltpu.VMEM((probes, cols), F32)],
        compiler_params=pltpu.CompilerParams(vmem_limit_bytes=56 * 2**20),
        cost_estimate=pl.CostEstimate(
            flops=4 * probes * rows * cols, bytes_accessed=4 * rows * cols, transcendentals=0
        ),
    )(*keep, *([current] + list(factors) + [carried]))


def pieces_kernel(solving, rhs, first, second, own, other, current, out, residual):
    @pl.when(pl.program_id(0) == 0)
    def _():
        totals = first[...].astype(F32) + second[...].astype(F32)
        residual[...] = (rhs[...] - totals).astype(BF16)

    for k, factor in enumerate((own, other)):
        piece = dot_t(residual[...], factor[...])
        out[k] = jnp.where(solving[0] == 1, piece, current[k].astype(F32)).astype(BF16)


def root_pieces(solving, rhs, first, second, factors, current):
    (rows, cols), probes, steps = factors[0].shape, rhs.shape[0], 3
    factor_spec = pl.BlockSpec((rows // steps, cols), lambda i: (i, 0))
    whole = pl.BlockSpec((probes, cols), lambda i: (0, 0))
    part = pl.BlockSpec((2, probes, rows // steps), lambda i: (0, 0, i))
    return pl.pallas_call(
        pieces_kernel,
        grid=(steps,),
        in_specs=[pl.BlockSpec(memory_space=pltpu.SMEM)] + [whole] * 3 + [factor_spec] * 2 + [part],
        out_specs=part,
        out_shape=jax.ShapeDtypeStruct(current.shape, BF16),
        scratch_shapes=[pltpu.VMEM((probes, cols), BF16)],
        compiler_params=pltpu.CompilerParams(vmem_limit_bytes=56 * 2**20),
        cost_estimate=pl.CostEstimate(
            flops=4 * probes * rows * cols, bytes_accessed=4 * rows * cols, transcendentals=0
        ),
    )(solving.astype(jnp.int32).reshape(1), rhs, first, second, *factors, current)


def sweep(rhs, current, forward, solve, split_rows, beside=lambda r, value: value):
    row_panel = lax.axis_index("row") // GROUP
    col_panel = lax.axis_index("col") // PAIR
    carried = jnp.zeros(rhs.shape, F32)
    first = second = jnp.zeros(rhs.shape, BF16)
    for r in range(PANELS - 1, -1, -1):
        ahead = None
        if r < PANELS - 1:
            terms = beside(r, forward(current, carried))
            down = [(r + 1, r, 0, r, r, 0)]
            if r == 1:
                down.append((3, 2, 0, 0, 0, 0))
            first = send(terms, down)
            if split_rows:
                second = send(terms, [(r + 1, r, 2, r, r, 0)])
            if r >= 1:
                ahead = send(current, [(r + 1, r + 1, 0, r, r - 1, 0)])
            carried = carried + first.astype(F32)
        current = solve((row_panel == r) & (col_panel == r), rhs, first, second, current)
        if r == PANELS - 1:
            current = beside(r, current)
        if ahead is not None:
            current = (current.astype(F32) + ahead.astype(F32)).astype(BF16)
        if r >= 1:
            straight = [(r, r, 0, r, r - 1, 0)]
            crossed = [(r, r, 0, r, r - 1, 1)]
            if r == 2:
                straight.append((3, 3, 0, 1, 0, 0))
                crossed.append((3, 3, 0, 3, 3, 1))
            if r == 1:
                straight.append((2, 2, 0, 0, 3, 0))
                crossed.append((2, 2, 0, 2, 2, 1))
            received = send(current, straight).astype(F32) + send(current, crossed).astype(F32)
            if r < PANELS - 1:
                terms = forward(current, carried)
                carried = carried + send(terms, [(r + 1, r, 0, r - 1, r - 1, 0)]).astype(F32)
            current = (current.astype(F32) + received).astype(BF16)
        else:
            received = [
                send(current, [(0, 0, 0, 0, 3, 0), (1, 1, 0, 0, 3, 0)]),
                send(current, [(0, 0, 0, 0, 3, 1), (1, 1, 0, 1, 1, 1)]),
                send(current, [(0, 0, 0, 0, 0, 1)]),
            ]
            current = sum([part.astype(F32) for part in received], current.astype(F32)).astype(BF16)
            received = send(current, [(0, 0, 0, 0, 1, 0), (0, 0, 0, 3, 2, 0), (1, 1, 0, 3, 2, 0)])
            current = (current.astype(F32) + received.astype(F32)).astype(BF16)
    return current


def per_device(root_factor, partials, pattern, coupling, child_factor, child_bits):
    layers = lax.axis_size("gz")
    rows_here, cols_here = root_factor.shape
    row_index = lax.axis_index("row")
    col_index = lax.axis_index("col")
    core = row_index % 2
    quarters = [[s * GROUP + j for j in range(GROUP)] for s in range(PANELS)]
    chips = [
        [g * ROWS + 2 * y + k for g in range(layers) for k in range(2)] for y in range(ROWS // 2)
    ]

    with jax.named_scope("mask"):
        swap = [(i, i ^ 1) for i in range(ROWS)]
        partner_factor = lax.ppermute(root_factor, "row", swap)
        partner_pattern = lax.ppermute(pattern, "row", swap)
        on_diagonal = row_index // GROUP == col_index // PAIR
        keep = [jnp.where(on_diagonal, 1, p).astype(F32) for p in (pattern, partner_pattern)]
        factors = [root_factor, partner_factor]

    with jax.named_scope("rhs"):
        probes_here = partials.shape[1]
        lanes = cols_here // 12
        pieces = partials[0].reshape(layers, 1, 2, 12, lanes)
        pieces = jnp.broadcast_to(pieces, (layers, ROWS // 2, 2, 12, lanes))
        pieces = lax.all_to_all(
            pieces.reshape(layers * ROWS, 12, lanes), ("gz", "row"), 0, 0, tiled=True
        )
        root_rhs = jnp.sum(pieces.astype(F32).reshape(layers, ROWS, 12, lanes), 0)
        root_rhs = root_rhs.astype(BF16).reshape(ROWS, 12 * lanes).astype(F32)

    child_here = child_factor[0]
    moved = {}

    def rows_of(half, flip):
        first = half * ROWS // 2
        return [(i, i ^ flip) for i in range(first, first + ROWS // 2)]

    def move_children(r, value):
        if r == 1:
            value, moved[0, 1], there = lax.optimization_barrier((value, moved[0, 1], moved[0, 2]))
            moved[0, 2] = there
            moved[0, 3] = lax.ppermute(there, "row", rows_of(0, 1))
        if r == 0:
            value, moved[0, 3] = lax.optimization_barrier((value, moved[0, 3]))
        if r == 3 or r == 0:
            half = 0 if r == 3 else 1
            value, here = lax.optimization_barrier((value, child_here))
            moved[half, 2] = lax.ppermute(here, "row", rows_of(half, 2))
            moved[half, 1] = lax.ppermute(here, "row", rows_of(half, 1))
        return value

    with jax.named_scope("root"):
        root_rows = sweep(
            root_rhs,
            jnp.zeros((2, root_rhs.shape[0], rows_here), BF16),
            lambda current, carried: root_terms(keep, factors, current, carried),
            lambda solving, rhs, first, second, current: root_pieces(
                solving, rhs, first, second, factors, current
            ),
            True,
            move_children,
        )

    with jax.named_scope("coupling"):
        root_rows, there = lax.optimization_barrier((root_rows, moved[1, 2]))
        moved[1, 3] = lax.ppermute(there, "row", rows_of(1, 1))
        own, other = root_rows[0], root_rows[1]
        by_core = jnp.stack([jnp.where(core == k, own, other) for k in range(2)])
        shared = jnp.broadcast_to(by_core[None], (layers,) + by_core.shape)
        shared = shared.reshape(layers * 2 * ROWS, rows_here)
        shared = lax.all_to_all(shared, ("gz", "row"), 0, 0, tiled=True, axis_index_groups=chips)
        root_all = shared.reshape(layers * 2, ROWS, rows_here).transpose(1, 0, 2)
        root_all = root_all.reshape(layers * 2 * ROWS, rows_here)
        terms = dot(root_all[:, : rows_here // 2], coupling[0]).astype(BF16)
        terms = lax.all_to_all(terms, "row", 0, 0, tiled=True, axis_index_groups=quarters)
        share = terms.shape[0] // GROUP
        terms = jnp.sum(terms.reshape(GROUP, share, -1).astype(F32), 0).astype(BF16)
        coupled = terms.astype(F32)
        for d in range(1, PANELS):
            parts = [((p + d) % PANELS, p, 0, p, p, 0) for p in range(PANELS)]
            coupled = coupled + send(terms, parts).astype(F32)
        bits = lax.dynamic_slice_in_dim(child_bits[0], row_index % GROUP * share, share, 0)
        child_rhs = (2 * bits - 1).astype(F32) - coupled

    with jax.named_scope("child"):
        blocks = [child_here] + [moved[0, flip] + moved[1, flip] for flip in (1, 2, 3)]
        rows = child_here.shape[0]

        def child_terms(current, carried):
            for i, block in enumerate(blocks):
                carried = carried + dot(current[:, i * rows : (i + 1) * rows], block)
            return carried.astype(BF16)

        def child_pieces(solving, rhs, first, second, current):
            residual = (rhs - first.astype(F32)).astype(BF16)
            piece = jnp.concatenate([dot_t(residual, block) for block in blocks], 1).astype(BF16)
            return jnp.where(solving, piece, current)

        child_rows = jnp.zeros((share, GROUP * rows), BF16)
        child_rows = sweep(child_rhs, child_rows, child_terms, child_pieces, False)
        child_rows = child_rows.reshape(share, 2, 2, -1)
        child_rows = jnp.where(core == 1, child_rows[:, :, ::-1], child_rows)
        child_rows = jnp.where(row_index % GROUP // 2 == 1, child_rows[:, ::-1], child_rows)
        child_rows = child_rows.reshape(share, GROUP, -1).transpose(1, 0, 2)
        child_rows = child_rows.reshape(GROUP * share, -1)
        child_rows = lax.all_to_all(child_rows, "row", 0, 0, tiled=True, axis_index_groups=quarters)
    return (root_all, child_rows[None])


def solution(mesh):
    placed = (
        P("row", "col"),
        P("gz", "row", "col"),
        P("row", "col"),
        P("gz", "row", "col"),
        P("gz", "row", "col"),
        P("gz", None, "col"),
    )
    return jax.shard_map(
        per_device,
        mesh=mesh,
        in_specs=placed,
        out_specs=(P(None, "row"), P("gz", None, "row")),
        check_vma=False,
    )
```

```python
import functools

import jax
import jax.numpy as jnp
from jax import lax
from jax.experimental import pallas as pl
from jax.experimental.pallas import tpu as pltpu
from jax.sharding import PartitionSpec as P

PANELS = 4
GROUP = 4
PAIR = 2
ROWS = PANELS * GROUP
COLS = PANELS * PAIR
GRID = ("row", "col")
F32 = jnp.float32
BF16 = jnp.bfloat16


def dot(a, b):
    return jnp.dot(a, b, preferred_element_type=F32)


def dot_t(a, b):
    return lax.dot_general(a, b, (((1,), (1,)), ((), ())), preferred_element_type=F32)


def send(value, moves):
    pairs = []
    for rows, to_rows, row_flip, cols, to_cols, col_flip in moves:
        for j in range(GROUP):
            for q in range(PAIR):
                source = (rows * GROUP + j) * COLS + cols * PAIR + q
                target = (to_rows * GROUP + (j ^ row_flip)) * COLS + to_cols * PAIR + (q ^ col_flip)
                pairs.append((source, target))
    return lax.ppermute(value, GRID, pairs)


def terms_kernel(count, masked, *refs):
    keep, refs = refs[: count * masked], refs[count * masked :]
    x, factors, (carried, terms, total) = refs[0], refs[1 : 1 + count], refs[1 + count :]
    step = pl.program_id(0)
    rows, cols = factors[0].shape
    width = rows if masked else cols

    @pl.when(step == 0)
    def _():
        total[...] = carried[...]

    for c in range(cols // width):
        part = slice(c * width, (c + 1) * width)
        for k in range(count):
            product = dot(x[k], factors[k][:, part])
            total[:, part] += keep[k][step, c] * product if masked else product

    @pl.when(step == pl.num_programs(0) - 1)
    def _():
        terms[...] = total[...].astype(BF16)


def terms_of(keep, steps, factors, current, carried):
    count, probes, (rows, cols) = len(factors), current.shape[1], factors[0].shape
    factor_spec = pl.BlockSpec((rows // steps, cols), lambda i: (i, 0))
    whole = pl.BlockSpec((probes, cols), lambda i: (0, 0))
    return pl.pallas_call(
        functools.partial(terms_kernel, count, len(keep) > 0),
        grid=(steps,),
        in_specs=[pl.BlockSpec(memory_space=pltpu.SMEM)] * len(keep)
        + [pl.BlockSpec((count, probes, rows // steps), lambda i: (0, 0, i))]
        + [factor_spec] * count
        + [whole],
        out_specs=whole,
        out_shape=jax.ShapeDtypeStruct((probes, cols), BF16),
        scratch_shapes=[pltpu.VMEM((probes, cols), F32)],
        compiler_params=pltpu.CompilerParams(vmem_limit_bytes=8 * 2**20),
        cost_estimate=pl.CostEstimate(
            flops=2 * count * probes * rows * cols,
            bytes_accessed=2 * count * rows * cols,
            transcendentals=0,
        ),
    )(*keep, current, *factors, carried)


def pieces_kernel(r, count, *refs):
    solving, rhs, refs = refs[0], refs[1], refs[2:]
    sums, factors = refs[: -count - 3], refs[-count - 3 : -3]
    current, out, residual = refs[-3:]

    @pl.when(pl.program_id(0) == 0)
    def _():
        left = rhs[...]
        if sums:
            left = left - sum([part[...].astype(F32) for part in sums[1:]], sums[0][...].astype(F32))
        residual[...] = left.astype(BF16)

    for k, factor in enumerate(factors):
        piece = dot_t(residual[...], factor[...])
        out[k] = jnp.where(solving[r] == 1, piece, current[k].astype(F32)).astype(BF16)


def pieces_of(solving, steps, factors, r, rhs, sums, current):
    (rows, cols), probes, count = factors[0].shape, rhs.shape[0], len(factors)
    factor_spec = pl.BlockSpec((rows // steps, cols), lambda i: (i, 0))
    whole = pl.BlockSpec((probes, cols), lambda i: (0, 0))
    part = pl.BlockSpec((count, probes, rows // steps), lambda i: (0, 0, i))
    return pl.pallas_call(
        functools.partial(pieces_kernel, r, count),
        grid=(steps,),
        in_specs=[pl.BlockSpec(memory_space=pltpu.SMEM)]
        + [whole] * (1 + len(sums))
        + [factor_spec] * count
        + [part],
        out_specs=part,
        out_shape=jax.ShapeDtypeStruct(current.shape, BF16),
        scratch_shapes=[pltpu.VMEM((probes, cols), BF16)],
        compiler_params=pltpu.CompilerParams(vmem_limit_bytes=8 * 2**20),
        cost_estimate=pl.CostEstimate(
            flops=2 * count * probes * rows * cols,
            bytes_accessed=2 * count * rows * cols,
            transcendentals=0,
        ),
    )(solving, rhs, *sums, *factors, current)


def sweep(rhs, current, forward, solve, split_rows, beside=lambda r, value: value):
    carried = jnp.zeros(rhs.shape, F32)
    for r in range(PANELS - 1, -1, -1):
        ahead, sums = None, []
        if r < PANELS - 1:
            terms = beside(r, forward(current, carried))
            down = [(r + 1, r, 0, r, r, 0)]
            if r == 1:
                down.append((3, 2, 0, 0, 0, 0))
            sums = [send(terms, down)]
            if split_rows:
                sums.append(send(terms, [(r + 1, r, 2, r, r, 0)]))
            if r >= 1:
                ahead = send(current, [(r + 1, r + 1, 0, r, r - 1, 0)])
            carried = carried + sums[0].astype(F32)
        current = solve(r, rhs, sums, current)
        if r == PANELS - 1:
            current = beside(r, current)
        if ahead is not None:
            current = (current.astype(F32) + ahead.astype(F32)).astype(BF16)
        if r >= 1:
            straight = [(r, r, 0, r, r - 1, 0)]
            crossed = [(r, r, 0, r, r - 1, 1)]
            if r == 2:
                straight.append((3, 3, 0, 1, 0, 0))
                crossed.append((3, 3, 0, 3, 3, 1))
            if r == 1:
                straight.append((2, 2, 0, 0, 3, 0))
                crossed.append((2, 2, 0, 2, 2, 1))
            received = send(current, straight).astype(F32) + send(current, crossed).astype(F32)
            if r < PANELS - 1:
                terms = forward(current, carried)
                carried = carried + send(terms, [(r + 1, r, 0, r - 1, r - 1, 0)]).astype(F32)
            current = (current.astype(F32) + received).astype(BF16)
        else:
            received = [
                send(current, [(0, 0, 0, 0, 3, 0), (1, 1, 0, 0, 3, 0)]),
                send(current, [(0, 0, 0, 0, 3, 1), (1, 1, 0, 1, 1, 1)]),
                send(current, [(0, 0, 0, 0, 0, 1)]),
            ]
            current = sum([part.astype(F32) for part in received], current.astype(F32)).astype(BF16)
            received = send(current, [(0, 0, 0, 0, 1, 0), (0, 0, 0, 3, 2, 0), (1, 1, 0, 3, 2, 0)])
            current = (current.astype(F32) + received.astype(F32)).astype(BF16)
    return current


def per_device(root_factor, partials, pattern, coupling, child_factor, child_bits):
    layers = lax.axis_size("gz")
    rows_here, cols_here = root_factor.shape
    row_index = lax.axis_index("row")
    col_index = lax.axis_index("col")
    core = row_index % 2
    quarters = [[s * GROUP + j for j in range(GROUP)] for s in range(PANELS)]
    chips = [
        [g * ROWS + 2 * y + k for g in range(layers) for k in range(2)] for y in range(ROWS // 2)
    ]

    with jax.named_scope("mask"):
        swap = [(i, i ^ 1) for i in range(ROWS)]
        partner_factor = lax.ppermute(root_factor, "row", swap)
        partner_pattern = lax.ppermute(pattern, "row", swap)
        on_diagonal = row_index // GROUP == col_index // PAIR
        keep = [jnp.where(on_diagonal, 1, p).astype(F32) for p in (pattern, partner_pattern)]
        factors = [root_factor, partner_factor]
        panel = jnp.arange(PANELS)
        solving = (panel == row_index // GROUP) & (panel == col_index // PAIR)
        solving = solving.astype(jnp.int32)

    with jax.named_scope("rhs"):
        lanes = cols_here // 12
        pieces = partials[0].reshape(layers, 1, 2, 12, lanes)
        pieces = jnp.broadcast_to(pieces, (layers, ROWS // 2, 2, 12, lanes))
        pieces = lax.all_to_all(
            pieces.reshape(layers * ROWS, 12, lanes), ("gz", "row"), 0, 0, tiled=True
        )
        root_rhs = jnp.sum(pieces.astype(F32).reshape(layers, ROWS, 12, lanes), 0)
        root_rhs = root_rhs.astype(BF16).reshape(ROWS, 12 * lanes).astype(F32)

    child_here = child_factor[0]
    moved = {}

    def rows_of(half, flip):
        first = half * ROWS // 2
        return [(i, i ^ flip) for i in range(first, first + ROWS // 2)]

    def move_children(r, value):
        if r == 1:
            value, moved[0, 1], there = lax.optimization_barrier((value, moved[0, 1], moved[0, 2]))
            moved[0, 2] = there
            moved[0, 3] = lax.ppermute(there, "row", rows_of(0, 1))
        if r == 0:
            value, moved[0, 3] = lax.optimization_barrier((value, moved[0, 3]))
        if r == 3 or r == 0:
            half = 0 if r == 3 else 1
            value, here = lax.optimization_barrier((value, child_here))
            moved[half, 2] = lax.ppermute(here, "row", rows_of(half, 2))
            moved[half, 1] = lax.ppermute(here, "row", rows_of(half, 1))
        return value

    with jax.named_scope("root"):
        root_rows = sweep(
            root_rhs,
            jnp.zeros((2, root_rhs.shape[0], rows_here), BF16),
            functools.partial(terms_of, keep, pattern.shape[0], factors),
            functools.partial(pieces_of, solving, pattern.shape[0], factors),
            True,
            move_children,
        )

    with jax.named_scope("coupling"):
        root_rows, there = lax.optimization_barrier((root_rows, moved[1, 2]))
        moved[1, 3] = lax.ppermute(there, "row", rows_of(1, 1))
        own, other = root_rows[0], root_rows[1]
        by_core = jnp.stack([jnp.where(core == k, own, other) for k in range(2)])
        shared = jnp.broadcast_to(by_core[None], (layers,) + by_core.shape)
        shared = shared.reshape(layers * 2 * ROWS, rows_here)
        shared = lax.all_to_all(shared, ("gz", "row"), 0, 0, tiled=True, axis_index_groups=chips)
        root_all = shared.reshape(layers * 2, ROWS, rows_here).transpose(1, 0, 2)
        root_all = root_all.reshape(layers * 2 * ROWS, rows_here)
        terms = dot(root_all[:, : rows_here // 2], coupling[0]).astype(BF16)
        terms = lax.all_to_all(terms, "row", 0, 0, tiled=True, axis_index_groups=quarters)
        share = terms.shape[0] // GROUP
        terms = jnp.sum(terms.reshape(GROUP, share, -1).astype(F32), 0).astype(BF16)
        coupled = terms.astype(F32)
        for d in range(1, PANELS):
            parts = [((p + d) % PANELS, p, 0, p, p, 0) for p in range(PANELS)]
            coupled = coupled + send(terms, parts).astype(F32)
        bits = lax.dynamic_slice_in_dim(child_bits[0], row_index % GROUP * share, share, 0)
        child_rhs = (2 * bits - 1).astype(F32) - coupled

    with jax.named_scope("child"):
        blocks = [child_here] + [moved[0, flip] + moved[1, flip] for flip in (1, 2, 3)]
        child_rows = sweep(
            child_rhs,
            jnp.zeros((GROUP, share, child_here.shape[0]), BF16),
            functools.partial(terms_of, [], 2, blocks),
            functools.partial(pieces_of, solving, 2, blocks),
            False,
        )
        child_rows = child_rows.reshape(2, 2, share, -1)
        child_rows = jnp.where(core == 1, child_rows[:, ::-1], child_rows)
        child_rows = jnp.where(row_index % GROUP // 2 == 1, child_rows[::-1], child_rows)
        child_rows = child_rows.reshape(GROUP * share, -1)
        child_rows = lax.all_to_all(child_rows, "row", 0, 0, tiled=True, axis_index_groups=quarters)
    return (root_all, child_rows[None])


def solution(mesh):
    placed = (
        P("row", "col"),
        P("gz", "row", "col"),
        P("row", "col"),
        P("gz", "row", "col"),
        P("gz", "row", "col"),
        P("gz", None, "col"),
    )
    return jax.shard_map(
        per_device,
        mesh=mesh,
        in_specs=placed,
        out_specs=(P(None, "row"), P("gz", None, "row")),
        check_vma=False,
    )
```

```python
import functools

import jax
import jax.numpy as jnp
from jax import lax
from jax.experimental import pallas as pl
from jax.experimental.pallas import tpu as pltpu
from jax.sharding import PartitionSpec as P

PANELS = 4
GROUP = 4
PAIR = 2
ROWS = PANELS * GROUP
COLS = PANELS * PAIR
GRID = ("row", "col")
F32 = jnp.float32
BF16 = jnp.bfloat16


def dot(a, b):
    return jnp.dot(a, b, preferred_element_type=F32)


def dot_t(a, b):
    return lax.dot_general(a, b, (((1,), (1,)), ((), ())), preferred_element_type=F32)


def send(value, moves):
    pairs = []
    for rows, to_rows, row_flip, cols, to_cols, col_flip in moves:
        for j in range(GROUP):
            for q in range(PAIR):
                source = (rows * GROUP + j) * COLS + cols * PAIR + q
                target = (to_rows * GROUP + (j ^ row_flip)) * COLS + to_cols * PAIR + (q ^ col_flip)
                pairs.append((source, target))
    return lax.ppermute(value, GRID, pairs)


def terms_kernel(count, masked, *refs):
    keep, refs = refs[: count * masked], refs[count * masked :]
    x, factors, (carried, terms, total) = refs[0], refs[1 : 1 + count], refs[1 + count :]
    step = pl.program_id(0)
    rows, cols = factors[0].shape
    width = rows if masked else cols

    @pl.when(step == 0)
    def _():
        total[...] = carried[...]

    for c in range(cols // width):
        part = slice(c * width, (c + 1) * width)
        for k in range(count):
            product = dot(x[k], factors[k][:, part])
            total[:, part] += keep[k][step, c] * product if masked else product

    @pl.when(step == pl.num_programs(0) - 1)
    def _():
        terms[...] = total[...].astype(BF16)


def terms_of(keep, steps, factors, current, carried):
    count, probes, (rows, cols) = len(factors), current.shape[1], factors[0].shape
    factor_spec = pl.BlockSpec((rows // steps, cols), lambda i: (i, 0))
    whole = pl.BlockSpec((probes, cols), lambda i: (0, 0))
    return pl.pallas_call(
        functools.partial(terms_kernel, count, len(keep) > 0),
        grid=(steps,),
        in_specs=[pl.BlockSpec(memory_space=pltpu.SMEM)] * len(keep)
        + [pl.BlockSpec((count, probes, rows // steps), lambda i: (0, 0, i))]
        + [factor_spec] * count
        + [whole],
        out_specs=whole,
        out_shape=jax.ShapeDtypeStruct((probes, cols), BF16),
        scratch_shapes=[pltpu.VMEM((probes, cols), F32)],
        compiler_params=pltpu.CompilerParams(vmem_limit_bytes=8 * 2**20),
        cost_estimate=pl.CostEstimate(
            flops=2 * count * probes * rows * cols,
            bytes_accessed=2 * count * rows * cols,
            transcendentals=0,
        ),
    )(*keep, current, *factors, carried)


def pieces_kernel(r, count, *refs):
    solving, rhs, refs = refs[0], refs[1], refs[2:]
    sums, factors = refs[: -count - 3], refs[-count - 3 : -3]
    current, out, residual = refs[-3:]

    @pl.when(pl.program_id(0) == 0)
    def _():
        left = rhs[...]
        if sums:
            left = left - sum([part[...].astype(F32) for part in sums[1:]], sums[0][...].astype(F32))
        residual[...] = left.astype(BF16)

    for k, factor in enumerate(factors):
        piece = dot_t(residual[...], factor[...])
        out[k] = jnp.where(solving[r] == 1, piece, current[k].astype(F32)).astype(BF16)


def pieces_of(solving, steps, factors, r, rhs, sums, current):
    (rows, cols), probes, count = factors[0].shape, rhs.shape[0], len(factors)
    factor_spec = pl.BlockSpec((rows // steps, cols), lambda i: (i, 0))
    whole = pl.BlockSpec((probes, cols), lambda i: (0, 0))
    part = pl.BlockSpec((count, probes, rows // steps), lambda i: (0, 0, i))
    return pl.pallas_call(
        functools.partial(pieces_kernel, r, count),
        grid=(steps,),
        in_specs=[pl.BlockSpec(memory_space=pltpu.SMEM)]
        + [whole] * (1 + len(sums))
        + [factor_spec] * count
        + [part],
        out_specs=part,
        out_shape=jax.ShapeDtypeStruct(current.shape, BF16),
        scratch_shapes=[pltpu.VMEM((probes, cols), BF16)],
        compiler_params=pltpu.CompilerParams(vmem_limit_bytes=8 * 2**20),
        cost_estimate=pl.CostEstimate(
            flops=2 * count * probes * rows * cols,
            bytes_accessed=2 * count * rows * cols,
            transcendentals=0,
        ),
    )(solving, rhs, *sums, *factors, current)


def sweep(rhs, current, forward, solve, split_rows, beside=lambda r, value: value):
    carried = jnp.zeros(rhs.shape, F32)
    for r in range(PANELS - 1, -1, -1):
        ahead, sums = None, []
        if r < PANELS - 1:
            terms = beside(r, forward(current, carried))
            down = [(r + 1, r, 0, r, r, 0)]
            if r == 1:
                down.append((3, 2, 0, 0, 0, 0))
            sums = [send(terms, down)]
            if split_rows:
                sums.append(send(terms, [(r + 1, r, 2, r, r, 0)]))
            elif r < PANELS - 2:
                sums.append(send(terms, [(r + 2, r, 0, r, r, 0)]))
            if r >= 1:
                ahead = send(current, [(r + 1, r + 1, 0, r, r - 1, 0)])
            carried = carried + sums[0].astype(F32)
        current = solve(r, rhs, sums, current)
        if r == PANELS - 1:
            current = beside(r, current)
        if ahead is not None:
            current = (current.astype(F32) + ahead.astype(F32)).astype(BF16)
        if r >= 1:
            straight = [(r, r, 0, r, r - 1, 0)]
            crossed = [(r, r, 0, r, r - 1, 1)]
            if r == 2:
                straight.append((3, 3, 0, 1, 0, 0))
                crossed.append((3, 3, 0, 3, 3, 1))
            if r == 1:
                straight.append((2, 2, 0, 0, 3, 0))
                crossed.append((2, 2, 0, 2, 2, 1))
            received = send(current, straight).astype(F32) + send(current, crossed).astype(F32)
            if r < PANELS - 1 and split_rows:
                terms = forward(current, carried)
                carried = carried + send(terms, [(r + 1, r, 0, r - 1, r - 1, 0)]).astype(F32)
            current = (current.astype(F32) + received).astype(BF16)
        else:
            received = [
                send(current, [(0, 0, 0, 0, 3, 0), (1, 1, 0, 0, 3, 0)]),
                send(current, [(0, 0, 0, 0, 3, 1), (1, 1, 0, 1, 1, 1)]),
                send(current, [(0, 0, 0, 0, 0, 1)]),
            ]
            current = sum([part.astype(F32) for part in received], current.astype(F32)).astype(BF16)
            received = send(current, [(0, 0, 0, 0, 1, 0), (0, 0, 0, 3, 2, 0), (1, 1, 0, 3, 2, 0)])
            current = (current.astype(F32) + received.astype(F32)).astype(BF16)
    return current


def per_device(root_factor, partials, pattern, coupling, child_factor, child_bits):
    layers = lax.axis_size("gz")
    rows_here, cols_here = root_factor.shape
    row_index = lax.axis_index("row")
    col_index = lax.axis_index("col")
    core = row_index % 2
    quarters = [[s * GROUP + j for j in range(GROUP)] for s in range(PANELS)]
    chips = [
        [g * ROWS + 2 * y + k for g in range(layers) for k in range(2)] for y in range(ROWS // 2)
    ]

    with jax.named_scope("mask"):
        swap = [(i, i ^ 1) for i in range(ROWS)]
        partner_factor = lax.ppermute(root_factor, "row", swap)
        partner_pattern = lax.ppermute(pattern, "row", swap)
        on_diagonal = row_index // GROUP == col_index // PAIR
        keep = [jnp.where(on_diagonal, 1, p).astype(F32) for p in (pattern, partner_pattern)]
        factors = [root_factor, partner_factor]
        panel = jnp.arange(PANELS)
        solving = (panel == row_index // GROUP) & (panel == col_index // PAIR)
        solving = solving.astype(jnp.int32)

    with jax.named_scope("rhs"):
        lanes = cols_here // 12
        pieces = partials[0].reshape(layers, 1, 2, 12, lanes)
        pieces = jnp.broadcast_to(pieces, (layers, ROWS // 2, 2, 12, lanes))
        pieces = lax.all_to_all(
            pieces.reshape(layers * ROWS, 12, lanes), ("gz", "row"), 0, 0, tiled=True
        )
        root_rhs = jnp.sum(pieces.astype(F32).reshape(layers, ROWS, 12, lanes), 0)
        root_rhs = root_rhs.astype(BF16).reshape(ROWS, 12 * lanes).astype(F32)

    child_here = child_factor[0]
    moved = {}

    def rows_of(half, flip):
        first = half * ROWS // 2
        return [(i, i ^ flip) for i in range(first, first + ROWS // 2)]

    def move_children(r, value):
        if r == 1:
            value, moved[0, 1], there = lax.optimization_barrier((value, moved[0, 1], moved[0, 2]))
            moved[0, 2] = there
            moved[0, 3] = lax.ppermute(there, "row", rows_of(0, 1))
        if r == 0:
            value, moved[0, 3] = lax.optimization_barrier((value, moved[0, 3]))
        if r == 3 or r == 0:
            half = 0 if r == 3 else 1
            value, here = lax.optimization_barrier((value, child_here))
            moved[half, 2] = lax.ppermute(here, "row", rows_of(half, 2))
            moved[half, 1] = lax.ppermute(here, "row", rows_of(half, 1))
        return value

    with jax.named_scope("root"):
        root_rows = sweep(
            root_rhs,
            jnp.zeros((2, root_rhs.shape[0], rows_here), BF16),
            functools.partial(terms_of, keep, pattern.shape[0], factors),
            functools.partial(pieces_of, solving, pattern.shape[0], factors),
            True,
            move_children,
        )

    with jax.named_scope("coupling"):
        root_rows, there = lax.optimization_barrier((root_rows, moved[1, 2]))
        moved[1, 3] = lax.ppermute(there, "row", rows_of(1, 1))
        own, other = root_rows[0], root_rows[1]
        by_core = jnp.stack([jnp.where(core == k, own, other) for k in range(2)])
        shared = jnp.broadcast_to(by_core[None], (layers,) + by_core.shape)
        shared = shared.reshape(layers * 2 * ROWS, rows_here)
        shared = lax.all_to_all(shared, ("gz", "row"), 0, 0, tiled=True, axis_index_groups=chips)
        root_all = shared.reshape(layers * 2, ROWS, rows_here).transpose(1, 0, 2)
        root_all = root_all.reshape(layers * 2 * ROWS, rows_here)
        terms = dot(root_all[:, : rows_here // 2], coupling[0]).astype(BF16)
        terms = lax.all_to_all(terms, "row", 0, 0, tiled=True, axis_index_groups=quarters)
        share = terms.shape[0] // GROUP
        terms = jnp.sum(terms.reshape(GROUP, share, -1).astype(F32), 0).astype(BF16)
        coupled = terms.astype(F32)
        for d in range(1, PANELS):
            parts = [((p + d) % PANELS, p, 0, p, p, 0) for p in range(PANELS)]
            coupled = coupled + send(terms, parts).astype(F32)
        bits = lax.dynamic_slice_in_dim(child_bits[0], row_index % GROUP * share, share, 0)
        child_rhs = (2 * bits - 1).astype(F32) - coupled

    with jax.named_scope("child"):
        blocks = [child_here] + [moved[0, flip] + moved[1, flip] for flip in (1, 2, 3)]
        rows = child_here.shape[0]
        solves = (row_index // GROUP, col_index // PAIR)

        def child_terms(current, carried):
            for i, block in enumerate(blocks):
                carried = carried + dot(current[:, i * rows : (i + 1) * rows], block)
            return carried.astype(BF16)

        def child_pieces(r, rhs, sums, current):
            for part in sums:
                rhs = rhs - part.astype(F32)
            residual = rhs.astype(BF16)
            piece = jnp.concatenate([dot_t(residual, block) for block in blocks], 1).astype(BF16)
            return jnp.where((solves[0] == r) & (solves[1] == r), piece, current)

        child_rows = jnp.zeros((share, GROUP * rows), BF16)
        child_rows = sweep(child_rhs, child_rows, child_terms, child_pieces, False)
        child_rows = child_rows.reshape(share, GROUP, rows).transpose(1, 0, 2)
        child_rows = child_rows.reshape(2, 2, share, -1)
        child_rows = jnp.where(core == 1, child_rows[:, ::-1], child_rows)
        child_rows = jnp.where(row_index % GROUP // 2 == 1, child_rows[::-1], child_rows)
        child_rows = child_rows.reshape(GROUP * share, -1)
        child_rows = lax.all_to_all(child_rows, "row", 0, 0, tiled=True, axis_index_groups=quarters)
    return (root_all, child_rows[None])


def solution(mesh):
    placed = (
        P("row", "col"),
        P("gz", "row", "col"),
        P("row", "col"),
        P("gz", "row", "col"),
        P("gz", "row", "col"),
        P("gz", None, "col"),
    )
    return jax.shard_map(
        per_device,
        mesh=mesh,
        in_specs=placed,
        out_specs=(P(None, "row"), P("gz", None, "row")),
        check_vma=False,
    )
```

```python
import functools

import jax
import jax.numpy as jnp
from jax import lax
from jax.experimental import pallas as pl
from jax.experimental.pallas import tpu as pltpu
from jax.sharding import PartitionSpec as P

PANELS = 4
GROUP = 4
PAIR = 2
ROWS = PANELS * GROUP
COLS = PANELS * PAIR
GRID = ("row", "col")
F32 = jnp.float32
BF16 = jnp.bfloat16


def dot(a, b):
    return jnp.dot(a, b, preferred_element_type=F32)


def dot_t(a, b):
    return lax.dot_general(a, b, (((1,), (1,)), ((), ())), preferred_element_type=F32)


def send(value, moves):
    pairs = []
    for rows, to_rows, row_flip, cols, to_cols, col_flip in moves:
        for j in range(GROUP):
            for q in range(PAIR):
                source = (rows * GROUP + j) * COLS + cols * PAIR + q
                target = (to_rows * GROUP + (j ^ row_flip)) * COLS + to_cols * PAIR + (q ^ col_flip)
                pairs.append((source, target))
    return lax.ppermute(value, GRID, pairs)


def terms_kernel(count, masked, *refs):
    keep, refs = refs[: count * masked], refs[count * masked :]
    x, factors, (carried, terms, total) = refs[0], refs[1 : 1 + count], refs[1 + count :]
    step = pl.program_id(0)
    rows, cols = factors[0].shape
    width = rows if masked else cols

    @pl.when(step == 0)
    def _():
        total[...] = carried[...]

    for c in range(cols // width):
        part = slice(c * width, (c + 1) * width)
        for k in range(count):
            product = dot(x[k], factors[k][:, part])
            total[:, part] += keep[k][step, c] * product if masked else product

    @pl.when(step == pl.num_programs(0) - 1)
    def _():
        terms[...] = total[...].astype(BF16)


def terms_of(keep, steps, factors, current, carried):
    count, probes, (rows, cols) = len(factors), current.shape[1], factors[0].shape
    factor_spec = pl.BlockSpec((rows // steps, cols), lambda i: (i, 0))
    whole = pl.BlockSpec((probes, cols), lambda i: (0, 0))
    return pl.pallas_call(
        functools.partial(terms_kernel, count, len(keep) > 0),
        grid=(steps,),
        in_specs=[pl.BlockSpec(memory_space=pltpu.SMEM)] * len(keep)
        + [pl.BlockSpec((count, probes, rows // steps), lambda i: (0, 0, i))]
        + [factor_spec] * count
        + [whole],
        out_specs=whole,
        out_shape=jax.ShapeDtypeStruct((probes, cols), BF16),
        scratch_shapes=[pltpu.VMEM((probes, cols), F32)],
        compiler_params=pltpu.CompilerParams(vmem_limit_bytes=8 * 2**20),
        cost_estimate=pl.CostEstimate(
            flops=2 * count * probes * rows * cols,
            bytes_accessed=2 * count * rows * cols,
            transcendentals=0,
        ),
    )(*keep, current, *factors, carried)


def pieces_kernel(r, count, *refs):
    solving, rhs, refs = refs[0], refs[1], refs[2:]
    sums, factors = refs[: -count - 3], refs[-count - 3 : -3]
    current, out, residual = refs[-3:]

    @pl.when(pl.program_id(0) == 0)
    def _():
        left = rhs[...]
        if sums:
            left = left - sum([part[...].astype(F32) for part in sums[1:]], sums[0][...].astype(F32))
        residual[...] = left.astype(BF16)

    for k, factor in enumerate(factors):
        piece = dot_t(residual[...], factor[...])
        out[k] = jnp.where(solving[r] == 1, piece, current[k].astype(F32)).astype(BF16)


def pieces_of(solving, steps, factors, r, rhs, sums, current):
    (rows, cols), probes, count = factors[0].shape, rhs.shape[0], len(factors)
    factor_spec = pl.BlockSpec((rows // steps, cols), lambda i: (i, 0))
    whole = pl.BlockSpec((probes, cols), lambda i: (0, 0))
    part = pl.BlockSpec((count, probes, rows // steps), lambda i: (0, 0, i))
    return pl.pallas_call(
        functools.partial(pieces_kernel, r, count),
        grid=(steps,),
        in_specs=[pl.BlockSpec(memory_space=pltpu.SMEM)]
        + [whole] * (1 + len(sums))
        + [factor_spec] * count
        + [part],
        out_specs=part,
        out_shape=jax.ShapeDtypeStruct(current.shape, BF16),
        scratch_shapes=[pltpu.VMEM((probes, cols), BF16)],
        compiler_params=pltpu.CompilerParams(vmem_limit_bytes=8 * 2**20),
        cost_estimate=pl.CostEstimate(
            flops=2 * count * probes * rows * cols,
            bytes_accessed=2 * count * rows * cols,
            transcendentals=0,
        ),
    )(solving, rhs, *sums, *factors, current)


def sweep(rhs, current, forward, solve, split_rows, beside=lambda r, value: value):
    carried = jnp.zeros(rhs.shape, F32)
    for r in range(PANELS - 1, -1, -1):
        ahead, sums = None, []
        if r < PANELS - 1:
            terms = beside(r, forward(current, carried))
            down = [(r + 1, r, 0, r, r, 0)]
            if r == 1:
                down.append((3, 2, 0, 0, 0, 0))
            sums = [send(terms, down)]
            if split_rows:
                sums.append(send(terms, [(r + 1, r, 2, r, r, 0)]))
            elif r < PANELS - 2:
                sums.append(send(terms, [(r + 2, r, 0, r, r, 0)]))
            if r >= 1:
                ahead = send(current, [(r + 1, r + 1, 0, r, r - 1, 0)])
            carried = carried + sums[0].astype(F32)
        current = solve(r, rhs, sums, current)
        if r == PANELS - 1:
            current = beside(r, current)
        if ahead is not None:
            current = (current.astype(F32) + ahead.astype(F32)).astype(BF16)
        if r >= 1:
            straight = [(r, r, 0, r, r - 1, 0)]
            crossed = [(r, r, 0, r, r - 1, 1)]
            if r == 2:
                straight.append((3, 3, 0, 1, 0, 0))
                crossed.append((3, 3, 0, 3, 3, 1))
            if r == 1:
                straight.append((2, 2, 0, 0, 3, 0))
                crossed.append((2, 2, 0, 2, 2, 1))
            received = send(current, straight).astype(F32) + send(current, crossed).astype(F32)
            if r < PANELS - 1 and split_rows:
                terms = forward(current, carried)
                carried = carried + send(terms, [(r + 1, r, 0, r - 1, r - 1, 0)]).astype(F32)
            current = (current.astype(F32) + received).astype(BF16)
        else:
            received = [
                send(current, [(0, 0, 0, 0, 3, 0), (1, 1, 0, 0, 3, 0)]),
                send(current, [(0, 0, 0, 0, 3, 1), (1, 1, 0, 1, 1, 1)]),
                send(current, [(0, 0, 0, 0, 0, 1)]),
            ]
            current = sum([part.astype(F32) for part in received], current.astype(F32)).astype(BF16)
            received = send(current, [(0, 0, 0, 0, 1, 0), (0, 0, 0, 3, 2, 0), (1, 1, 0, 3, 2, 0)])
            current = (current.astype(F32) + received.astype(F32)).astype(BF16)
    return current


def per_device(root_factor, partials, pattern, coupling, child_factor, child_bits):
    layers = lax.axis_size("gz")
    rows_here, cols_here = root_factor.shape
    row_index = lax.axis_index("row")
    col_index = lax.axis_index("col")
    core = row_index % 2
    quarters = [[s * GROUP + j for j in range(GROUP)] for s in range(PANELS)]
    chips = [
        [g * ROWS + 2 * y + k for g in range(layers) for k in range(2)] for y in range(ROWS // 2)
    ]

    with jax.named_scope("mask"):
        swap = [(i, i ^ 1) for i in range(ROWS)]
        partner_factor = lax.ppermute(root_factor, "row", swap)
        partner_pattern = lax.ppermute(pattern, "row", swap)
        on_diagonal = row_index // GROUP == col_index // PAIR
        keep = [jnp.where(on_diagonal, 1, p).astype(F32) for p in (pattern, partner_pattern)]
        factors = [root_factor, partner_factor]
        panel = jnp.arange(PANELS)
        solving = (panel == row_index // GROUP) & (panel == col_index // PAIR)
        solving = solving.astype(jnp.int32)

    with jax.named_scope("rhs"):
        lanes = cols_here // 12
        pieces = partials[0].reshape(layers, 1, 2, 12, lanes)
        pieces = jnp.broadcast_to(pieces, (layers, ROWS // 2, 2, 12, lanes))
        pieces = lax.all_to_all(
            pieces.reshape(layers * ROWS, 12, lanes), ("gz", "row"), 0, 0, tiled=True
        )
        root_rhs = jnp.sum(pieces.astype(F32).reshape(layers, ROWS, 12, lanes), 0)
        root_rhs = root_rhs.astype(BF16).reshape(ROWS, 12 * lanes).astype(F32)

    child_here = child_factor[0]
    moved = {}

    def rows_of(half, flip):
        first = half * ROWS // 2
        return [(i, i ^ flip) for i in range(first, first + ROWS // 2)]

    def move_children(r, value):
        if r == 1:
            value, moved[0, 1], there = lax.optimization_barrier((value, moved[0, 1], moved[0, 2]))
            moved[0, 2] = there
            moved[0, 3] = lax.ppermute(there, "row", rows_of(0, 1))
        if r == 0:
            value, moved[0, 3] = lax.optimization_barrier((value, moved[0, 3]))
        if r == 3 or r == 0:
            half = 0 if r == 3 else 1
            value, here = lax.optimization_barrier((value, child_here))
            moved[half, 2] = lax.ppermute(here, "row", rows_of(half, 2))
            moved[half, 1] = lax.ppermute(here, "row", rows_of(half, 1))
        return value

    with jax.named_scope("root"):
        root_rows = sweep(
            root_rhs,
            jnp.zeros((2, root_rhs.shape[0], rows_here), BF16),
            functools.partial(terms_of, keep, pattern.shape[0], factors),
            functools.partial(pieces_of, solving, pattern.shape[0], factors),
            True,
            move_children,
        )

    with jax.named_scope("coupling"):
        root_rows, there = lax.optimization_barrier((root_rows, moved[1, 2]))
        moved[1, 3] = lax.ppermute(there, "row", rows_of(1, 1))
        own, other = root_rows[0], root_rows[1]
        by_core = jnp.stack([jnp.where(core == k, own, other) for k in range(2)])
        shared = jnp.broadcast_to(by_core[None], (layers,) + by_core.shape)
        shared = shared.reshape(layers * 2 * ROWS, rows_here)
        shared = lax.all_to_all(shared, ("gz", "row"), 0, 0, tiled=True, axis_index_groups=chips)
        root_all = shared.reshape(layers * 2, ROWS, rows_here).transpose(1, 0, 2)
        root_all = root_all.reshape(layers * 2 * ROWS, rows_here)
        terms = dot(root_all[:, : rows_here // 2], coupling[0]).astype(BF16)
        terms = lax.all_to_all(terms, "row", 0, 0, tiled=True, axis_index_groups=quarters)
        share = terms.shape[0] // GROUP
        terms = jnp.sum(terms.reshape(GROUP, share, -1).astype(F32), 0).astype(BF16)
        coupled = terms.astype(F32)
        for d in range(1, PANELS):
            parts = [((p + d) % PANELS, p, 0, p, p, 0) for p in range(PANELS)]
            coupled = coupled + send(terms, parts).astype(F32)
        bits = lax.dynamic_slice_in_dim(child_bits[0], row_index % GROUP * share, share, 0)
        child_rhs = (2 * bits - 1).astype(F32) - coupled

    with jax.named_scope("child"):
        blocks = [child_here] + [moved[0, flip] + moved[1, flip] for flip in (1, 2, 3)]
        rows = child_here.shape[0]

        def child_terms(current, carried):
            for i, block in enumerate(blocks):
                carried = carried + dot(current[:, i * rows : (i + 1) * rows], block)
            return carried.astype(BF16)

        def child_pieces(r, rhs, sums, current):
            for part in sums:
                rhs = rhs - part.astype(F32)
            residual = rhs.astype(BF16)
            piece = jnp.concatenate([dot_t(residual, block) for block in blocks], 1).astype(BF16)
            return jnp.where(solving[r : r + 1].reshape(1, 1) == 1, piece, current)

        child_rows = jnp.zeros((share, GROUP * rows), BF16)
        child_rows = sweep(child_rhs, child_rows, child_terms, child_pieces, False)
        child_rows = child_rows.reshape(share, GROUP, rows).transpose(1, 0, 2)
        child_rows = child_rows.reshape(2, 2, share, -1)
        child_rows = jnp.where(core == 1, child_rows[:, ::-1], child_rows)
        child_rows = jnp.where(row_index % GROUP // 2 == 1, child_rows[::-1], child_rows)
        child_rows = child_rows.reshape(GROUP * share, -1)
        child_rows = lax.all_to_all(child_rows, "row", 0, 0, tiled=True, axis_index_groups=quarters)
    return (root_all, child_rows[None])


def solution(mesh):
    placed = (
        P("row", "col"),
        P("gz", "row", "col"),
        P("row", "col"),
        P("gz", "row", "col"),
        P("gz", "row", "col"),
        P("gz", None, "col"),
    )
    return jax.shard_map(
        per_device,
        mesh=mesh,
        in_specs=placed,
        out_specs=(P(None, "row"), P("gz", None, "row")),
        check_vma=False,
    )
```

```python
import functools

import jax
import jax.numpy as jnp
from jax import lax
from jax.experimental import pallas as pl
from jax.experimental.pallas import tpu as pltpu
from jax.sharding import PartitionSpec as P

PANELS = 4
GROUP = 4
PAIR = 2
ROWS = PANELS * GROUP
COLS = PANELS * PAIR
GRID = ("row", "col")
F32 = jnp.float32
BF16 = jnp.bfloat16


def dot(a, b):
    return jnp.dot(a, b, preferred_element_type=F32)


def dot_t(a, b):
    return lax.dot_general(a, b, (((1,), (1,)), ((), ())), preferred_element_type=F32)


def send(value, moves):
    pairs = []
    for rows, to_rows, row_flip, cols, to_cols, col_flip in moves:
        for j in range(GROUP):
            for q in range(PAIR):
                source = (rows * GROUP + j) * COLS + cols * PAIR + q
                target = (to_rows * GROUP + (j ^ row_flip)) * COLS + to_cols * PAIR + (q ^ col_flip)
                pairs.append((source, target))
    return lax.ppermute(value, GRID, pairs)


def terms_kernel(count, masked, *refs):
    keep, refs = refs[: count * masked], refs[count * masked :]
    x, factors, (carried, terms, total) = refs[0], refs[1 : 1 + count], refs[1 + count :]
    step = pl.program_id(0)
    rows, cols = factors[0].shape
    width = rows if masked else cols

    @pl.when(step == 0)
    def _():
        total[...] = carried[...]

    for c in range(cols // width):
        part = slice(c * width, (c + 1) * width)
        for k in range(count):
            product = dot(x[k], factors[k][:, part])
            total[:, part] += keep[k][step, c] * product if masked else product

    @pl.when(step == pl.num_programs(0) - 1)
    def _():
        terms[...] = total[...].astype(BF16)


def terms_of(keep, steps, factors, current, carried):
    count, probes, (rows, cols) = len(factors), current.shape[1], factors[0].shape
    factor_spec = pl.BlockSpec((rows // steps, cols), lambda i: (i, 0))
    whole = pl.BlockSpec((probes, cols), lambda i: (0, 0))
    return pl.pallas_call(
        functools.partial(terms_kernel, count, len(keep) > 0),
        grid=(steps,),
        in_specs=[pl.BlockSpec(memory_space=pltpu.SMEM)] * len(keep)
        + [pl.BlockSpec((count, probes, rows // steps), lambda i: (0, 0, i))]
        + [factor_spec] * count
        + [whole],
        out_specs=whole,
        out_shape=jax.ShapeDtypeStruct((probes, cols), BF16),
        scratch_shapes=[pltpu.VMEM((probes, cols), F32)],
        compiler_params=pltpu.CompilerParams(vmem_limit_bytes=8 * 2**20),
        cost_estimate=pl.CostEstimate(
            flops=2 * count * probes * rows * cols,
            bytes_accessed=2 * count * rows * cols,
            transcendentals=0,
        ),
    )(*keep, current, *factors, carried)


def pieces_kernel(r, count, *refs):
    solving, rhs, refs = refs[0], refs[1], refs[2:]
    sums, factors = refs[: -count - 3], refs[-count - 3 : -3]
    current, out, residual = refs[-3:]

    @pl.when(pl.program_id(0) == 0)
    def _():
        left = rhs[...]
        if sums:
            left = left - sum([part[...].astype(F32) for part in sums[1:]], sums[0][...].astype(F32))
        residual[...] = left.astype(BF16)

    for k, factor in enumerate(factors):
        piece = dot_t(residual[...], factor[...])
        out[k] = jnp.where(solving[r] == 1, piece, current[k].astype(F32)).astype(BF16)


def pieces_of(solving, steps, factors, r, rhs, sums, current):
    (rows, cols), probes, count = factors[0].shape, rhs.shape[0], len(factors)
    factor_spec = pl.BlockSpec((rows // steps, cols), lambda i: (i, 0))
    whole = pl.BlockSpec((probes, cols), lambda i: (0, 0))
    part = pl.BlockSpec((count, probes, rows // steps), lambda i: (0, 0, i))
    return pl.pallas_call(
        functools.partial(pieces_kernel, r, count),
        grid=(steps,),
        in_specs=[pl.BlockSpec(memory_space=pltpu.SMEM)]
        + [whole] * (1 + len(sums))
        + [factor_spec] * count
        + [part],
        out_specs=part,
        out_shape=jax.ShapeDtypeStruct(current.shape, BF16),
        scratch_shapes=[pltpu.VMEM((probes, cols), BF16)],
        compiler_params=pltpu.CompilerParams(vmem_limit_bytes=8 * 2**20),
        cost_estimate=pl.CostEstimate(
            flops=2 * count * probes * rows * cols,
            bytes_accessed=2 * count * rows * cols,
            transcendentals=0,
        ),
    )(solving, rhs, *sums, *factors, current)


def sweep(rhs, current, forward, solve, split_rows, beside=lambda r, value: value):
    carried = jnp.zeros(rhs.shape, F32)
    for r in range(PANELS - 1, -1, -1):
        ahead, sums = None, []
        if r < PANELS - 1:
            terms = beside(r, forward(current, carried))
            down = [(r + 1, r, 0, r, r, 0)]
            if r == 1:
                down.append((3, 2, 0, 0, 0, 0))
            sums = [send(terms, down)]
            if split_rows:
                sums.append(send(terms, [(r + 1, r, 2, r, r, 0)]))
            elif r < PANELS - 2:
                sums.append(send(terms, [(r + 2, r, 0, r, r, 0)]))
            if r >= 1:
                ahead = send(current, [(r + 1, r + 1, 0, r, r - 1, 0)])
            carried = carried + sums[0].astype(F32)
        current = solve(r, rhs, sums, current)
        if r == PANELS - 1:
            current = beside(r, current)
        if ahead is not None:
            current = (current.astype(F32) + ahead.astype(F32)).astype(BF16)
        if r >= 1:
            straight = [(r, r, 0, r, r - 1, 0)]
            crossed = [(r, r, 0, r, r - 1, 1)]
            if r == 2:
                straight.append((3, 3, 0, 1, 0, 0))
                crossed.append((3, 3, 0, 3, 3, 1))
            if r == 1:
                straight.append((2, 2, 0, 0, 3, 0))
                crossed.append((2, 2, 0, 2, 2, 1))
            received = send(current, straight).astype(F32) + send(current, crossed).astype(F32)
            if r < PANELS - 1 and split_rows:
                terms = forward(current, carried)
                carried = carried + send(terms, [(r + 1, r, 0, r - 1, r - 1, 0)]).astype(F32)
            current = (current.astype(F32) + received).astype(BF16)
        else:
            received = [
                send(current, [(0, 0, 0, 0, 3, 0), (1, 1, 0, 0, 3, 0)]),
                send(current, [(0, 0, 0, 0, 3, 1), (1, 1, 0, 1, 1, 1)]),
                send(current, [(0, 0, 0, 0, 0, 1)]),
            ]
            current = sum([part.astype(F32) for part in received], current.astype(F32)).astype(BF16)
            received = send(current, [(0, 0, 0, 0, 1, 0), (0, 0, 0, 3, 2, 0), (1, 1, 0, 3, 2, 0)])
            current = (current.astype(F32) + received.astype(F32)).astype(BF16)
    return current


def per_device(root_factor, partials, pattern, coupling, child_factor, child_bits):
    layers = lax.axis_size("gz")
    rows_here, cols_here = root_factor.shape
    row_index = lax.axis_index("row")
    col_index = lax.axis_index("col")
    core = row_index % 2
    quarters = [[s * GROUP + j for j in range(GROUP)] for s in range(PANELS)]
    chips = [
        [g * ROWS + 2 * y + k for g in range(layers) for k in range(2)] for y in range(ROWS // 2)
    ]

    with jax.named_scope("mask"):
        swap = [(i, i ^ 1) for i in range(ROWS)]
        partner_factor = lax.ppermute(root_factor, "row", swap)
        partner_pattern = lax.ppermute(pattern, "row", swap)
        on_diagonal = row_index // GROUP == col_index // PAIR
        keep = [jnp.where(on_diagonal, 1, p).astype(F32) for p in (pattern, partner_pattern)]
        factors = [root_factor, partner_factor]
        panel = jnp.arange(PANELS)
        solving = (panel == row_index // GROUP) & (panel == col_index // PAIR)
        solving = solving.astype(jnp.int32)

    with jax.named_scope("rhs"):
        lanes = cols_here // 12
        pieces = partials[0].reshape(layers, 1, 2, 12, lanes)
        pieces = jnp.broadcast_to(pieces, (layers, ROWS // 2, 2, 12, lanes))
        pieces = lax.all_to_all(
            pieces.reshape(layers * ROWS, 12, lanes), ("gz", "row"), 0, 0, tiled=True
        )
        root_rhs = jnp.sum(pieces.astype(F32).reshape(layers, ROWS, 12, lanes), 0)
        root_rhs = root_rhs.astype(BF16).reshape(ROWS, 12 * lanes).astype(F32)

    child_here = child_factor[0]
    moved = {}

    def rows_of(half, flip):
        first = half * ROWS // 2
        return [(i, i ^ flip) for i in range(first, first + ROWS // 2)]

    def move_children(r, value):
        if r == 1:
            value, moved[0, 1], there = lax.optimization_barrier((value, moved[0, 1], moved[0, 2]))
            moved[0, 2] = there
            moved[0, 3] = lax.ppermute(there, "row", rows_of(0, 1))
        if r == 0:
            value, moved[0, 3] = lax.optimization_barrier((value, moved[0, 3]))
        if r == 3 or r == 0:
            half = 0 if r == 3 else 1
            value, here = lax.optimization_barrier((value, child_here))
            moved[half, 2] = lax.ppermute(here, "row", rows_of(half, 2))
            moved[half, 1] = lax.ppermute(here, "row", rows_of(half, 1))
        return value

    with jax.named_scope("root"):
        root_rows = sweep(
            root_rhs,
            jnp.zeros((2, root_rhs.shape[0], rows_here), BF16),
            functools.partial(terms_of, keep, pattern.shape[0], factors),
            functools.partial(pieces_of, solving, pattern.shape[0], factors),
            True,
            move_children,
        )

    with jax.named_scope("coupling"):
        root_rows, there = lax.optimization_barrier((root_rows, moved[1, 2]))
        moved[1, 3] = lax.ppermute(there, "row", rows_of(1, 1))
        own, other = root_rows[0], root_rows[1]
        by_core = jnp.stack([jnp.where(core == k, own, other) for k in range(2)])
        shared = jnp.broadcast_to(by_core[None], (layers,) + by_core.shape)
        shared = shared.reshape(layers * 2 * ROWS, rows_here)
        shared = lax.all_to_all(shared, ("gz", "row"), 0, 0, tiled=True, axis_index_groups=chips)
        root_all = shared.reshape(layers * 2, ROWS, rows_here).transpose(1, 0, 2)
        root_all = root_all.reshape(layers * 2 * ROWS, rows_here)
        terms = dot(root_all[:, : rows_here // 2], coupling[0]).astype(BF16)
        terms = lax.all_to_all(terms, "row", 0, 0, tiled=True, axis_index_groups=quarters)
        share = terms.shape[0] // GROUP
        terms = jnp.sum(terms.reshape(GROUP, share, -1).astype(F32), 0).astype(BF16)
        coupled = terms.astype(F32)
        for d in range(1, PANELS):
            parts = [((p + d) % PANELS, p, 0, p, p, 0) for p in range(PANELS)]
            coupled = coupled + send(terms, parts).astype(F32)
        bits = lax.dynamic_slice_in_dim(child_bits[0], row_index % GROUP * share, share, 0)
        child_rhs = (2 * bits - 1).astype(F32) - coupled

    with jax.named_scope("child"):
        blocks = [moved[0, flip] + moved[1, flip] for flip in (1, 2, 3)]
        blocks = [jnp.where(row_index < 0, blocks[0], child_here)] + blocks
        rows = child_here.shape[0]

        def child_terms(current, carried):
            for i, block in enumerate(blocks):
                carried = carried + dot(current[:, i * rows : (i + 1) * rows], block)
            return carried.astype(BF16)

        def child_pieces(r, rhs, sums, current):
            for part in sums:
                rhs = rhs - part.astype(F32)
            residual = rhs.astype(BF16)
            piece = jnp.concatenate([dot_t(residual, block) for block in blocks], 1).astype(BF16)
            return jnp.where(solving[r : r + 1].reshape(1, 1) == 1, piece, current)

        child_rows = jnp.zeros((share, GROUP * rows), BF16)
        child_rows = sweep(child_rhs, child_rows, child_terms, child_pieces, False)
        child_rows = child_rows.reshape(share, GROUP, rows).transpose(1, 0, 2)
        child_rows = child_rows.reshape(2, 2, share, -1)
        child_rows = jnp.where(core == 1, child_rows[:, ::-1], child_rows)
        child_rows = jnp.where(row_index % GROUP // 2 == 1, child_rows[::-1], child_rows)
        child_rows = child_rows.reshape(GROUP * share, -1)
        child_rows = lax.all_to_all(child_rows, "row", 0, 0, tiled=True, axis_index_groups=quarters)
    return (root_all, child_rows[None])


def solution(mesh):
    placed = (
        P("row", "col"),
        P("gz", "row", "col"),
        P("row", "col"),
        P("gz", "row", "col"),
        P("gz", "row", "col"),
        P("gz", None, "col"),
    )
    return jax.shard_map(
        per_device,
        mesh=mesh,
        in_specs=placed,
        out_specs=(P(None, "row"), P("gz", None, "row")),
        check_vma=False,
    )
```

```python
import functools

import jax
import jax.numpy as jnp
from jax import lax
from jax.experimental import pallas as pl
from jax.experimental.pallas import tpu as pltpu
from jax.sharding import PartitionSpec as P

PANELS = 4
GROUP = 4
PAIR = 2
ROWS = PANELS * GROUP
COLS = PANELS * PAIR
GRID = ("row", "col")
F32 = jnp.float32
BF16 = jnp.bfloat16


def dot(a, b):
    return jnp.dot(a, b, preferred_element_type=F32)


def dot_t(a, b):
    return lax.dot_general(a, b, (((1,), (1,)), ((), ())), preferred_element_type=F32)


def send(value, moves):
    pairs = []
    for rows, to_rows, row_flip, cols, to_cols, col_flip in moves:
        for j in range(GROUP):
            for q in range(PAIR):
                source = (rows * GROUP + j) * COLS + cols * PAIR + q
                target = (to_rows * GROUP + (j ^ row_flip)) * COLS + to_cols * PAIR + (q ^ col_flip)
                pairs.append((source, target))
    return lax.ppermute(value, GRID, pairs)


def terms_kernel(count, masked, *refs):
    keep, refs = refs[: count * masked], refs[count * masked :]
    x, factors, (carried, terms, total) = refs[0], refs[1 : 1 + count], refs[1 + count :]
    step = pl.program_id(0)
    rows, cols = factors[0].shape
    width = rows if masked else cols

    @pl.when(step == 0)
    def _():
        total[...] = carried[...]

    for c in range(cols // width):
        part = slice(c * width, (c + 1) * width)
        for k in range(count):
            product = dot(x[k], factors[k][:, part])
            total[:, part] += keep[k][step, c] * product if masked else product

    @pl.when(step == pl.num_programs(0) - 1)
    def _():
        terms[...] = total[...].astype(BF16)


def terms_of(keep, steps, factors, current, carried):
    count, probes, (rows, cols) = len(factors), current.shape[1], factors[0].shape
    factor_spec = pl.BlockSpec((rows // steps, cols), lambda i: (i, 0))
    whole = pl.BlockSpec((probes, cols), lambda i: (0, 0))
    return pl.pallas_call(
        functools.partial(terms_kernel, count, len(keep) > 0),
        grid=(steps,),
        in_specs=[pl.BlockSpec(memory_space=pltpu.SMEM)] * len(keep)
        + [pl.BlockSpec((count, probes, rows // steps), lambda i: (0, 0, i))]
        + [factor_spec] * count
        + [whole],
        out_specs=whole,
        out_shape=jax.ShapeDtypeStruct((probes, cols), BF16),
        scratch_shapes=[pltpu.VMEM((probes, cols), F32)],
        compiler_params=pltpu.CompilerParams(vmem_limit_bytes=8 * 2**20),
        cost_estimate=pl.CostEstimate(
            flops=2 * count * probes * rows * cols,
            bytes_accessed=2 * count * rows * cols,
            transcendentals=0,
        ),
    )(*keep, current, *factors, carried)


def pieces_kernel(r, count, *refs):
    solving, rhs, refs = refs[0], refs[1], refs[2:]
    sums, factors = refs[: -count - 3], refs[-count - 3 : -3]
    current, out, residual = refs[-3:]

    @pl.when(pl.program_id(0) == 0)
    def _():
        left = rhs[...]
        if sums:
            left = left - sum([part[...].astype(F32) for part in sums[1:]], sums[0][...].astype(F32))
        residual[...] = left.astype(BF16)

    for k, factor in enumerate(factors):
        piece = dot_t(residual[...], factor[...])
        out[k] = jnp.where(solving[r] == 1, piece, current[k].astype(F32)).astype(BF16)


def pieces_of(solving, steps, factors, r, rhs, sums, current):
    (rows, cols), probes, count = factors[0].shape, rhs.shape[0], len(factors)
    factor_spec = pl.BlockSpec((rows // steps, cols), lambda i: (i, 0))
    whole = pl.BlockSpec((probes, cols), lambda i: (0, 0))
    part = pl.BlockSpec((count, probes, rows // steps), lambda i: (0, 0, i))
    return pl.pallas_call(
        functools.partial(pieces_kernel, r, count),
        grid=(steps,),
        in_specs=[pl.BlockSpec(memory_space=pltpu.SMEM)]
        + [whole] * (1 + len(sums))
        + [factor_spec] * count
        + [part],
        out_specs=part,
        out_shape=jax.ShapeDtypeStruct(current.shape, BF16),
        scratch_shapes=[pltpu.VMEM((probes, cols), BF16)],
        compiler_params=pltpu.CompilerParams(vmem_limit_bytes=8 * 2**20),
        cost_estimate=pl.CostEstimate(
            flops=2 * count * probes * rows * cols,
            bytes_accessed=2 * count * rows * cols,
            transcendentals=0,
        ),
    )(solving, rhs, *sums, *factors, current)


def sweep(rhs, current, forward, solve, split_rows, beside=lambda r, value: value):
    carried = jnp.zeros(rhs.shape, F32)
    for r in range(PANELS - 1, -1, -1):
        ahead, sums = None, []
        if r < PANELS - 1:
            terms = beside(r, forward(current, carried))
            down = [(r + 1, r, 0, r, r, 0)]
            if r == 1:
                down.append((3, 2, 0, 0, 0, 0))
            sums = [send(terms, down)]
            if split_rows:
                sums.append(send(terms, [(r + 1, r, 2, r, r, 0)]))
            elif r < PANELS - 2:
                sums.append(send(terms, [(r + 2, r, 0, r, r, 0)]))
            if r >= 1:
                ahead = send(current, [(r + 1, r + 1, 0, r, r - 1, 0)])
            carried = carried + sums[0].astype(F32)
        current = solve(r, rhs, sums, current)
        if r == PANELS - 1:
            current = beside(r, current)
        if ahead is not None:
            current = (current.astype(F32) + ahead.astype(F32)).astype(BF16)
        if r >= 1:
            straight = [(r, r, 0, r, r - 1, 0)]
            crossed = [(r, r, 0, r, r - 1, 1)]
            if r == 2:
                straight.append((3, 3, 0, 1, 0, 0))
                crossed.append((3, 3, 0, 3, 3, 1))
            if r == 1:
                straight.append((2, 2, 0, 0, 3, 0))
                crossed.append((2, 2, 0, 2, 2, 1))
            received = send(current, straight).astype(F32) + send(current, crossed).astype(F32)
            if r < PANELS - 1 and split_rows:
                terms = forward(current, carried)
                carried = carried + send(terms, [(r + 1, r, 0, r - 1, r - 1, 0)]).astype(F32)
            current = (current.astype(F32) + received).astype(BF16)
        else:
            received = [
                send(current, [(0, 0, 0, 0, 3, 0), (1, 1, 0, 0, 3, 0)]),
                send(current, [(0, 0, 0, 0, 3, 1), (1, 1, 0, 1, 1, 1)]),
                send(current, [(0, 0, 0, 0, 0, 1)]),
            ]
            current = sum([part.astype(F32) for part in received], current.astype(F32)).astype(BF16)
            received = send(current, [(0, 0, 0, 0, 1, 0), (0, 0, 0, 3, 2, 0), (1, 1, 0, 3, 2, 0)])
            current = (current.astype(F32) + received.astype(F32)).astype(BF16)
    return current


def per_device(root_factor, partials, pattern, coupling, child_factor, child_bits):
    layers = lax.axis_size("gz")
    rows_here, cols_here = root_factor.shape
    row_index = lax.axis_index("row")
    col_index = lax.axis_index("col")
    core = row_index % 2
    quarters = [[s * GROUP + j for j in range(GROUP)] for s in range(PANELS)]
    chips = [
        [g * ROWS + 2 * y + k for g in range(layers) for k in range(2)] for y in range(ROWS // 2)
    ]

    with jax.named_scope("mask"):
        swap = [(i, i ^ 1) for i in range(ROWS)]
        partner_factor = lax.ppermute(root_factor, "row", swap)
        partner_pattern = lax.ppermute(pattern, "row", swap)
        on_diagonal = row_index // GROUP == col_index // PAIR
        keep = [jnp.where(on_diagonal, 1, p).astype(F32) for p in (pattern, partner_pattern)]
        factors = [root_factor, partner_factor]
        panel = jnp.arange(PANELS)
        solving = (panel == row_index // GROUP) & (panel == col_index // PAIR)
        solving = solving.astype(jnp.int32)

    with jax.named_scope("rhs"):
        lanes = cols_here // 12
        pieces = partials[0].reshape(layers, 1, 2, 12, lanes)
        pieces = jnp.broadcast_to(pieces, (layers, ROWS // 2, 2, 12, lanes))
        pieces = lax.all_to_all(
            pieces.reshape(layers * ROWS, 12, lanes), ("gz", "row"), 0, 0, tiled=True
        )
        root_rhs = jnp.sum(pieces.astype(F32).reshape(layers, ROWS, 12, lanes), 0)
        root_rhs = root_rhs.astype(BF16).reshape(ROWS, 12 * lanes).astype(F32)

    child_here = child_factor[0]
    moved = {}

    def rows_of(half, flip):
        first = half * ROWS // 2
        return [(i, i ^ flip) for i in range(first, first + ROWS // 2)]

    def move_children(r, value):
        if r == 1:
            value, moved[1], there = lax.optimization_barrier((value, moved[1], moved[0, 2]))
            moved[0, 2] = there
            moved[0, 3] = lax.ppermute(there, "row", rows_of(0, 1))
        if r == 0:
            value, moved[0, 3] = lax.optimization_barrier((value, moved[0, 3]))
        if r == 3 or r == 0:
            half = 0 if r == 3 else 1
            value, here = lax.optimization_barrier((value, child_here))
            moved[half, 2] = lax.ppermute(here, "row", rows_of(half, 2))
            if r == 3:
                moved[1] = lax.ppermute(here, "row", swap)
        return value

    with jax.named_scope("root"):
        root_rows = sweep(
            root_rhs,
            jnp.zeros((2, root_rhs.shape[0], rows_here), BF16),
            functools.partial(terms_of, keep, pattern.shape[0], factors),
            functools.partial(pieces_of, solving, pattern.shape[0], factors),
            True,
            move_children,
        )

    with jax.named_scope("coupling"):
        root_rows, there = lax.optimization_barrier((root_rows, moved[1, 2]))
        moved[1, 3] = lax.ppermute(there, "row", rows_of(1, 1))
        own, other = root_rows[0], root_rows[1]
        by_core = jnp.stack([jnp.where(core == k, own, other) for k in range(2)])
        shared = jnp.broadcast_to(by_core[None], (layers,) + by_core.shape)
        shared = shared.reshape(layers * 2 * ROWS, rows_here)
        shared = lax.all_to_all(shared, ("gz", "row"), 0, 0, tiled=True, axis_index_groups=chips)
        root_all = shared.reshape(layers * 2, ROWS, rows_here).transpose(1, 0, 2)
        root_all = root_all.reshape(layers * 2 * ROWS, rows_here)
        terms = dot(root_all[:, : rows_here // 2], coupling[0]).astype(BF16)
        terms = lax.all_to_all(terms, "row", 0, 0, tiled=True, axis_index_groups=quarters)
        share = terms.shape[0] // GROUP
        terms = jnp.sum(terms.reshape(GROUP, share, -1).astype(F32), 0).astype(BF16)
        coupled = terms.astype(F32)
        for d in range(1, PANELS):
            parts = [((p + d) % PANELS, p, 0, p, p, 0) for p in range(PANELS)]
            coupled = coupled + send(terms, parts).astype(F32)
        bits = lax.dynamic_slice_in_dim(child_bits[0], row_index % GROUP * share, share, 0)
        child_rhs = (2 * bits - 1).astype(F32) - coupled

    with jax.named_scope("child"):
        blocks = [moved[0, flip] + moved[1, flip] for flip in (2, 3)]
        blocks = [jnp.where(row_index < 0, blocks[0], near) for near in (child_here, moved[1])] + blocks
        rows = child_here.shape[0]

        def child_terms(current, carried):
            for i, block in enumerate(blocks):
                carried = carried + dot(current[:, i * rows : (i + 1) * rows], block)
            return carried.astype(BF16)

        def child_pieces(r, rhs, sums, current):
            for part in sums:
                rhs = rhs - part.astype(F32)
            residual = rhs.astype(BF16)
            piece = jnp.concatenate([dot_t(residual, block) for block in blocks], 1).astype(BF16)
            return jnp.where(solving[r : r + 1].reshape(1, 1) == 1, piece, current)

        child_rows = jnp.zeros((share, GROUP * rows), BF16)
        child_rows = sweep(child_rhs, child_rows, child_terms, child_pieces, False)
        child_rows = child_rows.reshape(share, GROUP, rows).transpose(1, 0, 2)
        child_rows = child_rows.reshape(2, 2, share, -1)
        child_rows = jnp.where(core == 1, child_rows[:, ::-1], child_rows)
        child_rows = jnp.where(row_index % GROUP // 2 == 1, child_rows[::-1], child_rows)
        child_rows = child_rows.reshape(GROUP * share, -1)
        child_rows = lax.all_to_all(child_rows, "row", 0, 0, tiled=True, axis_index_groups=quarters)
    return (root_all, child_rows[None])


def solution(mesh):
    placed = (
        P("row", "col"),
        P("gz", "row", "col"),
        P("row", "col"),
        P("gz", "row", "col"),
        P("gz", "row", "col"),
        P("gz", None, "col"),
    )
    return jax.shard_map(
        per_device,
        mesh=mesh,
        in_specs=placed,
        out_specs=(P(None, "row"), P("gz", None, "row")),
        check_vma=False,
    )
```
